256 devices in a mesh: seq: 32 (over y, x, core), exp: 8 (over z).
Axes of the slice: x: 4, y: 4, z: 8, core: 2. Of those that a mesh axis runs over, the one named last changes fastest.
Arguments:
- mixer_input: bfloat16 [32768, 8192], P('seq', 'exp'), may hold values from -6 to 6
- log_decay: float32 [128, 32768], P('exp', 'seq'), may hold values from -1 to 0, as said below
- b_rows: bfloat16 [32768, 128], P('seq'), may hold values from -0.23925781 to 0.23925781
- c_rows: bfloat16 [32768, 128], P('seq'), may hold values from -0.23925781 to 0.23925781
- skip_gain: float32 [128], P('exp'), may hold values from 0.5 to 1.5
- grad_out: bfloat16 [32768, 8192], P('seq', 'exp'), may hold values from -6 to 6
Outputs:
- mixer_out: bfloat16 [32768, 8192], P('seq', 'exp')
- grad_input: bfloat16 [32768, 8192], P('seq', 'exp')
- grad_log_decay: float32 [128, 32768], P('exp', 'seq')
- grad_b: float32 [32768, 128], P(('seq', 'exp'))
- grad_c: float32 [32768, 128], P(('seq', 'exp'))
The draws below stay inside these ranges and needn't reach their ends.
Inputs may be any that keep to these rules, and one draw needn't show every extreme that they name: log_decay is negative everywhere.
All inputs are finite; a program needn't handle non-finite values.
Results may differ from the reference program's by a relative error of at most 0.02.
Values sent between devices are 32-bit elements; how exact they have to be, the bound alone decides.
A program may use at most 192 MiB of HBM per device.

```python
import jax
import jax.numpy as jnp
from jax import lax

HEAD_TOTAL = 128
HEAD_DIM = 64
STATE = 128
SPAN = 256
L_DEV = 1024
SEQUENCE_LENGTH = 32768
WIDTH = 8192
N_EXP = 8


def draw_log_decay(key, part):
    key = jax.random.fold_in(key, 11)
    random_subkeys = jax.random.split(key, 7)
    slow_share = 0.5
    slow_heads = jax.random.uniform(random_subkeys[0], (HEAD_TOTAL, 1)) < slow_share
    slow_rate = jnp.exp(jax.random.uniform(random_subkeys[1], (HEAD_TOTAL, 1), minval=jnp.log(0.05), maxval=jnp.log(0.5))) / SEQUENCE_LENGTH
    fast_rate = jnp.exp(jax.random.uniform(random_subkeys[2], (HEAD_TOTAL, 1), minval=jnp.log(1.0 / 50.0), maxval=jnp.log(1.0 / 30.0)))
    base_rate = jnp.where(slow_heads, slow_rate, fast_rate)
    block_factor = 2.0 ** jax.random.uniform(random_subkeys[3], (HEAD_TOTAL, SEQUENCE_LENGTH // L_DEV, 1), minval=-0.5, maxval=0.5)
    roughness = jax.random.uniform(random_subkeys[4], (HEAD_TOTAL, SEQUENCE_LENGTH // L_DEV, L_DEV), minval=0.5, maxval=1.5)
    every_decay_rate = (base_rate[:, :, None] * block_factor * roughness).reshape(HEAD_TOTAL, SEQUENCE_LENGTH)
    spike_positions = jax.random.randint(random_subkeys[5], (3,), 0, SEQUENCE_LENGTH)
    spike_mask = jnp.any(jnp.arange(SEQUENCE_LENGTH)[None, :] == spike_positions[:, None], axis=0)
    spike_depth = jax.random.uniform(random_subkeys[6], (HEAD_TOTAL, SEQUENCE_LENGTH), minval=0.22, maxval=0.5)
    return -(every_decay_rate + jnp.where(spike_mask[None, :], spike_depth, 0.0)).astype(jnp.float32)


def steps_of(own_key, shape, cuts, low, high):
    gain, own = 1.0, jax.random.fold_in(own_key, 6)
    for dim, parts in cuts:
        draws = jnp.exp(jax.random.uniform(jax.random.fold_in(own, dim), (parts,), jnp.float32, low / len(cuts), high / len(cuts)))
        gain = gain * jnp.repeat(draws, shape[dim] // parts).reshape([-1 if axis == dim else 1 for axis in range(len(shape))])
    return gain


def noise(stream_key, dims, scale, bound, cuts=(), kind=jnp.bfloat16):
    result = scale * jax.random.normal(stream_key, dims, jnp.float32)
    if cuts:
        result = result * steps_of(stream_key, dims, cuts, -0.22, 0.18)
    return jnp.clip(result, -bound, bound).astype(kind)


def setup_inputs(seed: int = 0) -> dict:
    key_list = jax.random.split(jax.random.key(seed), 7)
    return {
        "mixer_input": noise(key_list[0], (SEQUENCE_LENGTH, WIDTH), 1.0, 6.0, ((0, 32), (1, 8))),
        "log_decay": draw_log_decay(jax.random.fold_in(key_list[6], 71), 0),
        "b_rows": noise(key_list[2], (SEQUENCE_LENGTH, STATE), 0.04, 0.23925781, ((0, 32),)),
        "c_rows": noise(key_list[3], (SEQUENCE_LENGTH, STATE), 0.04, 0.23925781, ((0, 32),)),
        "skip_gain": jnp.clip(0.5 + 1.0 * jax.random.uniform(key_list[4], (HEAD_TOTAL,), jnp.float32) ** steps_of(key_list[4], (HEAD_TOTAL,), ((0, 8),), -0.2, 0.2), 0.5, 1.5),
        "grad_out": noise(key_list[5], (SEQUENCE_LENGTH, WIDTH), 1.0, 6.0, ((0, 32), (1, 8))),
    }


def lowp(value):
    return value.astype(jnp.bfloat16)

def mixer_blocks(inputs_x, log_rates, b_in, c_in, skip_part, entering):
    length, channels = inputs_x.shape
    head_count = log_rates.shape[0]
    head_size = channels // head_count
    state_size = b_in.shape[1]
    block_count = length // SPAN
    split_x = inputs_x.reshape(block_count, SPAN, head_count, head_size)
    split_rates = log_rates.reshape(head_count, block_count, SPAN).transpose(1, 0, 2)
    split_b = b_in.reshape(block_count, SPAN, state_size)
    split_c = c_in.reshape(block_count, SPAN, state_size)
    causal = jnp.arange(SPAN)[:, None] >= jnp.arange(SPAN)[None, :]

    def advance(running, pieces):
        piece_x, piece_rates, piece_b, piece_c = pieces
        cumul = jnp.cumsum(piece_rates, axis=1)
        spread = jnp.where(causal[None], cumul[:, :, None] - cumul[:, None, :], -jnp.inf)
        match_cb = jnp.dot(lowp(piece_c), lowp(piece_b).T, preferred_element_type=jnp.float32)
        weights_ts = jnp.exp(spread) * match_cb[None]
        inner_y = jnp.einsum('hts,shp->thp', lowp(weights_ts), lowp(piece_x), preferred_element_type=jnp.float32)
        from_state = jnp.einsum('tn,hnp->thp', lowp(piece_c), lowp(running), preferred_element_type=jnp.float32)
        from_state = from_state * jnp.exp(cumul).T[:, :, None]
        tail_weight = jnp.exp(cumul[:, -1:] - cumul)
        scaled_x = piece_x * tail_weight.T[:, :, None]
        fresh = jnp.einsum('sn,shp->hnp', lowp(piece_b), lowp(scaled_x), preferred_element_type=jnp.float32)
        updated = jnp.exp(cumul[:, -1])[:, None, None] * running + fresh
        output_y = inner_y + from_state + skip_part[None, :, None] * piece_x
        return (updated, output_y)
    final, outputs = lax.scan(jax.checkpoint(advance), entering, (split_x, split_rates, split_b, split_c))
    return (outputs.reshape(length, channels), final)

def reference(mixer_input, log_decay, b_rows, c_rows, skip_gain, grad_out):
    head_group = HEAD_TOTAL // N_EXP
    group_width = head_group * HEAD_DIM
    b_full = b_rows.astype(jnp.float32)
    c_full = c_rows.astype(jnp.float32)
    zero_state = jnp.zeros((head_group, STATE, HEAD_DIM), jnp.float32)

    def one_group(index):
        inputs_x = lax.dynamic_slice_in_dim(mixer_input, index * group_width, group_width, 1).astype(jnp.float32)
        cotangent = lax.dynamic_slice_in_dim(grad_out, index * group_width, group_width, 1).astype(jnp.float32)
        rates = lax.dynamic_slice_in_dim(log_decay, index * head_group, head_group, 0)
        gains = lax.dynamic_slice_in_dim(skip_gain, index * head_group, head_group, 0)

        def forward_map(part_x, part_rates, part_b, part_c):
            return mixer_blocks(part_x, part_rates, part_b, part_c, gains, zero_state)
        primal_out, pullback = jax.vjp(forward_map, inputs_x, rates, b_full, c_full)
        grads = pullback((cotangent, jnp.zeros_like(zero_state)))
        return (primal_out[0].astype(jnp.bfloat16), grads[0].astype(jnp.bfloat16), grads[1].astype(jnp.float32), grads[2].astype(jnp.float32), grads[3].astype(jnp.float32))
    stacked = lax.map(one_group, jnp.arange(N_EXP, dtype=jnp.int32))
    mixer_out = stacked[0].transpose(1, 0, 2).reshape(SEQUENCE_LENGTH, WIDTH)
    grad_input = stacked[1].transpose(1, 0, 2).reshape(SEQUENCE_LENGTH, WIDTH)
    grad_log_decay = stacked[2].reshape(HEAD_TOTAL, SEQUENCE_LENGTH)
    grad_b = lax.optimization_barrier(jnp.sum(stacked[3], axis=0))
    grad_c = lax.optimization_barrier(jnp.sum(stacked[4], axis=0))
    return (mixer_out, grad_input, grad_log_decay, grad_b, grad_c)
```

```python
import functools

import jax
import jax.numpy as jnp
from jax import lax
from jax.experimental import pallas as pl
from jax.experimental.pallas import tpu as pltpu
from jax.sharding import PartitionSpec as P

F32 = jnp.float32
BF16 = jnp.bfloat16
MESH = pl.DeviceIdType.MESH
HEAD = 64
LANES = 128


def dot(a, b, ca, cb):
    return lax.dot_general(a, b, (((ca,), (cb,)), ((), ())), preferred_element_type=F32)


def nn(a, b):
    return dot(a, b, 1, 0)


def nt(a, b):
    return dot(a, b, 1, 1)


def tn(a, b):
    return dot(a, b, 0, 0)


def iota(shape, axis):
    return lax.broadcasted_iota(jnp.int32, shape, axis)


def pieces(value, count, axis):
    out = []
    for _ in range(count):
        part = value.astype(BF16)
        value = value - part.astype(F32)
        out.append(part)
    return jnp.concatenate(out, axis=axis)


def kernel(chips, ring, x_ref, ld_ref, b_ref, c_ref, skip_ref, dy_ref,
           y_ref, dx_ref, gld_ref, gb_ref, gc_ref,
           xs, ds, a_exp, inv_exp, gmat, hmat, sp, tp, mm, mt, dcs, dbs, bnd,
           spread, parts_a, parts_i, rows, lam, tri_s, skipe,
           state, grad, th, tb, lamh, lamp, pf, pb, cmf, cmb, rf, rb, esf, esb,
           ref_, reb, p2f, p2b, pef, peb, rsbuf,
           pair_s, pair_r, a2a_s, a2a_r, rs_s, rs_r):
    seq = lax.axis_index("seq")
    z = lax.axis_index("exp")
    core = lax.rem(seq, 2)
    chip = seq // 2
    other = 1 - core
    partner = (chip * 2 + other, z)
    heads = ld_ref.shape[0]
    length, width = x_ref.shape
    nc = ring
    q = length // nc
    state_n = b_ref.shape[1]
    pr = state_n // chips
    half = width // 2
    lb = half // LANES
    kh = nc * heads
    far = ring // 2

    def chip_dev(p):
        return (p * 2 + core, z)

    def at_chip(d):
        return lax.rem(chip + d, chips)

    barrier = pltpu.get_barrier_semaphore()
    pl.semaphore_signal(barrier, inc=1, device_id=partner, device_id_type=MESH)
    for d in range(1, chips):
        pl.semaphore_signal(barrier, inc=1, device_id=chip_dev(at_chip(d)), device_id_type=MESH)
    z_dn = lax.rem(z + ring - 1, ring)
    z_up = lax.rem(z + 1, ring)
    pl.semaphore_signal(barrier, inc=1, device_id=(seq, z_dn), device_id_type=MESH)
    pl.semaphore_signal(barrier, inc=1, device_id=(seq, z_up), device_id_type=MESH)

    def remote(src, dst, s_sem, r_sem, dev):
        return pltpu.make_async_remote_copy(
            src_ref=src, dst_ref=dst, send_sem=s_sem, recv_sem=r_sem,
            device_id=dev, device_id_type=MESH)

    stacked = jnp.concatenate([ld_ref[:, c * q:(c + 1) * q] for c in range(nc)], axis=0)
    tri = (iota((q, q), 0) >= iota((q, q), 1)).astype(BF16)
    cum = nt(jnp.concatenate([tri] * 3, axis=1), pieces(stacked, 3, 1))
    tri_s[...] = jnp.concatenate([tri] * 3, axis=0)
    rho = cum[q // 2 - 1:q // 2, :]
    tot = cum[q - 1:q, :]
    shifted = cum - rho
    parts_a[...] = pieces(jnp.exp(shifted), 2, 1)
    parts_i[...] = pieces(jnp.exp(-shifted), 2, 1)
    one = (lax.rem(iota((kh, width), 0), heads) == iota((kh, width), 1) // HEAD).astype(BF16)
    spread[...] = jnp.concatenate([one, one], axis=0)
    own_row = iota((nc, kh), 1) // heads == iota((nc, kh), 0)
    pair_rows = jnp.concatenate(
        [jnp.where(own_row, jnp.exp(rho), 0.0), jnp.where(own_row, jnp.exp(tot - rho), 0.0)], axis=0)
    rows[...] = nn(pieces(pair_rows, 3, 1), jnp.concatenate([one, one, one], axis=0))
    both = rows[0:nc, :] * rows[nc:2 * nc, :]
    total = both[0:1, :]
    for c in range(1, nc):
        total = total * both[c:c + 1, :]
    lam[...] = total
    for h in range(2):
        for r in range(lb):
            lamh[h, r:r + 1, :] = total[:, h * half + r * LANES:h * half + (r + 1) * LANES]
    head_one = (iota((heads, width), 1) // HEAD == iota((heads, width), 0)).astype(BF16)
    skipe[...] = nn(pieces(skip_ref[...], 3, 1), jnp.concatenate([head_one] * 3, axis=0))

    pl.semaphore_wait(barrier, chips + 2)
    send_lam = remote(lamh.at[other], lamp, pair_s.at[0], pair_r.at[0], partner)
    send_lam.start()

    def rows_of(c):
        return pl.ds(pl.multiple_of(c * q, q), q)

    lane_chunk = lax.rem(iota((q, 2 * kh), 1), kh) // heads

    state[...] = jnp.zeros_like(state)
    grad[...] = jnp.zeros_like(grad)

    def fwd_local(c, _):
        inv = nn(jnp.where(lane_chunk == c, parts_i[...], jnp.zeros((), BF16)), spread[...])
        inv_exp[c] = inv
        scaled = (x_ref[rows_of(c), :].astype(F32) * inv).astype(BF16)
        xs[c] = scaled
        got = tn(b_ref[rows_of(c), :], scaled)
        gmat[c] = got
        f = rows[pl.ds(c, 1), :]
        g = rows[pl.ds(nc + c, 1), :]
        state[...] = g * (f * state[...] + got)
        return 0

    def bwd_local(i, _):
        c = nc - 1 - i
        a = nn(jnp.where(lane_chunk == c, parts_a[...], jnp.zeros((), BF16)), spread[...])
        a_exp[c] = a
        scaled = (dy_ref[rows_of(c), :].astype(F32) * a).astype(BF16)
        ds[c] = scaled
        got = tn(c_ref[rows_of(c), :], scaled)
        hmat[c] = got
        f = rows[pl.ds(c, 1), :]
        g = rows[pl.ds(nc + c, 1), :]
        grad[...] = f * (g * grad[...] + got)
        return 0

    def to_halves(src, dst):
        for h in range(2):
            for r in range(lb):
                lo = h * half + r * LANES
                dst[h, r] = src[:, lo:lo + LANES].reshape(chips, pr, LANES)

    def lane_row(ref, r):
        return ref[r:r + 1, :].reshape(1, 1, LANES)

    lax.fori_loop(0, nc, fwd_local, 0)
    to_halves(state, th)
    send_pf = remote(th.at[other], pf, pair_s.at[1], pair_r.at[1], partner)
    send_pf.start()
    lax.fori_loop(0, nc, bwd_local, 0)
    to_halves(grad, tb)
    send_pb = remote(tb.at[other], pb, pair_s.at[2], pair_r.at[2], partner)
    send_pb.start()

    first = core == 0

    send_lam.wait_recv()
    send_pf.wait_recv()
    for r in range(lb):
        lo_, lp_ = lamh[core, r:r + 1, :].reshape(1, 1, LANES), lane_row(lamp, r)
        mine, theirs = th[core, r], pf[r]
        chip_t = jnp.where(first, lp_, 1.0) * mine + jnp.where(first, 1.0, lo_) * theirs
        cmf[:, r * pr:(r + 1) * pr, :] = chip_t
        cmf[:, lb * pr + r:lb * pr + r + 1, :] = jnp.broadcast_to(lo_ * lp_, (chips, 1, LANES))

    def exchange(src_of, dst, sems, base):
        out = []
        for d in range(1, chips):
            p = at_chip(d)
            out.append(remote(src_of.at[p], dst.at[chip], a2a_s.at[base, d], a2a_r.at[base, d], chip_dev(p)))
        for copy in out:
            copy.start()
        dst[chip] = src_of[chip]
        return out

    go_f = exchange(cmf, rf, None, 0)

    send_pb.wait_recv()
    for r in range(lb):
        lo_, lp_ = lamh[core, r:r + 1, :].reshape(1, 1, LANES), lane_row(lamp, r)
        mine, theirs = tb[core, r], pb[r]
        cmb[:, r * pr:(r + 1) * pr, :] = (
            jnp.where(first, 1.0, lp_) * mine + jnp.where(first, lo_, 1.0) * theirs)
    go_b = exchange(cmb, rb, None, 1)

    lower = iota((q, q), 0) >= iota((q, q), 1)
    upper = iota((q, q), 0) <= iota((q, q), 1)

    def inner(c, _):
        bb, cc = b_ref[rows_of(c), :], c_ref[rows_of(c), :]
        mm[c] = jnp.where(lower, nt(cc, bb), 0.0).astype(BF16)
        mt[c] = jnp.where(upper, nt(bb, cc), 0.0).astype(BF16)
        dm = jnp.where(lower, nt(ds[c], xs[c]), 0.0).astype(BF16)
        dcs[c] = nn(dm, bb)
        dbs[c] = tn(dm, cc)
        return 0

    lax.fori_loop(0, nc // 2, inner, 0)

    for copy in go_f:
        copy.wait_recv()
    run = [jnp.zeros((pr, LANES), F32) for _ in range(lb)]
    for p in range(chips):
        for r in range(lb):
            esf[p, r * pr:(r + 1) * pr, :] = run[r]
            run[r] = rf[p, lb * pr + r:lb * pr + r + 1, :] * run[r] + rf[p, r * pr:(r + 1) * pr, :]
    ret_f = exchange(esf, ref_, None, 2)

    for copy in go_b:
        copy.wait_recv()
    run = [jnp.zeros((pr, LANES), F32) for _ in range(lb)]
    for p in reversed(range(chips)):
        for r in range(lb):
            esb[p, r * pr:(r + 1) * pr, :] = run[r]
            run[r] = rf[p, lb * pr + r:lb * pr + r + 1, :] * run[r] + rb[p, r * pr:(r + 1) * pr, :]
    ret_b = exchange(esb, reb, None, 3)

    lax.fori_loop(nc // 2, nc, inner, 0)

    def place(dst, r, lane_half, value):
        lo = pl.multiple_of(lane_half * half + r * LANES, LANES)
        dst[:, pl.ds(lo, LANES)] = value.reshape(state_n, LANES)

    for copy in ret_f:
        copy.wait_recv()
    for r in range(lb):
        lo_, lp_ = lamh[core, r:r + 1, :].reshape(1, 1, LANES), lane_row(lamp, r)
        enter = ref_[:, r * pr:(r + 1) * pr, :]
        later = jnp.where(first, lo_, lp_) * enter + jnp.where(first, th[core, r], pf[r])
        p2f[r] = jnp.where(first, later, enter)
        place(state, r, core, jnp.where(first, enter, later))
    send_2f = remote(p2f, pef, pair_s.at[3], pair_r.at[3], partner)
    send_2f.start()

    for copy in ret_b:
        copy.wait_recv()
    for r in range(lb):
        lo_, lp_ = lamh[core, r:r + 1, :].reshape(1, 1, LANES), lane_row(lamp, r)
        enter = reb[:, r * pr:(r + 1) * pr, :]
        earlier = jnp.where(first, lp_, lo_) * enter + jnp.where(first, pb[r], tb[core, r])
        p2b[r] = jnp.where(first, enter, earlier)
        place(grad, r, core, jnp.where(first, earlier, enter))
    send_2b = remote(p2b, peb, pair_s.at[4], pair_r.at[4], partner)
    send_2b.start()

    send_2f.wait_recv()
    for r in range(lb):
        place(state, r, other, pef[r])

    def fwd_state(c, _):
        f = rows[pl.ds(c, 1), :]
        g = rows[pl.ds(nc + c, 1), :]
        entering = f * state[...]
        sp[c] = entering.astype(BF16)
        leaving = entering + gmat[c]
        gmat[c] = leaving
        state[...] = g * leaving
        return 0

    lax.fori_loop(0, nc, fwd_state, 0)

    hq = q // 2

    def rs_copy(t, way, step, src):
        to = (seq, z_dn if way == 0 else z_up)
        dst = rsbuf.at[t, way, step]
        if step == 0:
            dst = dst.at[pl.ds(way * hq, hq)]
        return remote(src, dst, rs_s.at[t, way, step], rs_r.at[t, way, step], to)

    def chunk_at(way, step):
        gap = far - step
        return lax.rem(z + (ring - gap if way == 0 else gap), ring)

    started = {}

    def rs_start(t, own):
        for way in range(2):
            src = own.at[chunk_at(way, 0), pl.ds(way * hq, hq)]
            started[t, way, 0] = rs_copy(t, way, 0, src)
            started[t, way, 0].start()

    def rs_next(t, own, step):
        for way in range(2):
            started[t, way, step - 1].wait_recv()
            k = chunk_at(way, step)
            if step == 1:
                lo = way * hq
                rsbuf[t, way, 0, lo:lo + hq, :] += own[k, lo:lo + hq, :]
                lo = hq - lo
                rsbuf[t, way, 0, lo:lo + hq, :] = own[k, lo:lo + hq, :]
            else:
                rsbuf[t, way, step - 1] += own[k]
            started[t, way, step] = rs_copy(t, way, step, rsbuf.at[t, way, step - 1])
            started[t, way, step].start()

    def rs_end(t, own, out):
        for way in range(2):
            started[t, way, far - 1].wait_recv()
        last = rsbuf[t, 0, far - 1] + rsbuf[t, 1, far - 1]
        if far == 1:
            raise ValueError("ring")
        out[...] = own[z] + last

    def dc_chunk(i, _):
        c = lax.rem(z + far + i, ring)
        dcs[c] += nt(ds[c], sp[c])
        return 0

    def db_chunk(i, _):
        c = lax.rem(z + far + i, ring)
        dbs[c] += nt(xs[c], tp[c])
        return 0

    dc_chunk(0, 0)
    rs_start(0, dcs)
    lax.fori_loop(1, nc, dc_chunk, 0)

    send_2b.wait_recv()
    for r in range(lb):
        place(grad, r, other, peb[r])

    def bwd_state(i, _):
        c = nc - 1 - i
        f = rows[pl.ds(c, 1), :]
        g = rows[pl.ds(nc + c, 1), :]
        later = g * grad[...]
        low = later.astype(BF16)
        tp[c] = low
        bnd[pl.ds(c, 1), :] = jnp.sum(low.astype(F32) * gmat[c], axis=0, keepdims=True)
        grad[...] = f * (later + hmat[c])
        return 0

    lax.fori_loop(0, nc, bwd_state, 0)
    rs_next(0, dcs, 1)
    db_chunk(0, 0)
    rs_start(1, dbs)
    lax.fori_loop(1, nc, db_chunk, 0)

    last_row = iota((q, width), 0) == q - 1

    def outputs(c, _):
        x_c, d_c = xs[c], ds[c]
        acc_y = nn(jnp.concatenate([mm[c], c_ref[rows_of(c), :]], axis=1),
                   jnp.concatenate([x_c, sp[c]], axis=0))
        acc_x = nn(jnp.concatenate([mt[c], b_ref[rows_of(c), :]], axis=1),
                   jnp.concatenate([d_c, tp[c]], axis=0))
        gain = skipe[...]
        y_ref[rows_of(c), :] = (a_exp[c] * acc_y + gain * x_ref[rows_of(c), :].astype(F32)).astype(BF16)
        dx_ref[rows_of(c), :] = (inv_exp[c] * acc_x + gain * dy_ref[rows_of(c), :].astype(F32)).astype(BF16)
        diff = d_c.astype(F32) * acc_y - x_c.astype(F32) * acc_x
        diff = diff + jnp.where(last_row, bnd[pl.ds(c, 1), :], 0.0)
        hi = diff.astype(BF16)
        lo = (diff - hi.astype(F32)).astype(BF16)
        per_head = nt(head_one, hi) + nt(head_one, lo)
        gld_ref[:, rows_of(c)] = nn(pieces(per_head, 3, 1), tri_s[...])
        return 0

    done = 0
    for step in range(1, far):
        upto = nc * step // far
        lax.fori_loop(done, upto, outputs, 0)
        done = upto
        if step + 1 < far:
            rs_next(0, dcs, step + 1)
        rs_next(1, dbs, step)
    lax.fori_loop(done, nc, outputs, 0)
    rs_end(0, dcs, gc_ref)
    rs_end(1, dbs, gb_ref)

    for copy in [send_lam, send_pf, send_pb, send_2f, send_2b, *go_f, *go_b, *ret_f, *ret_b,
                 *started.values()]:
        copy.wait_send()


def body(chips, ring, mixer_input, log_decay, b_rows, c_rows, skip_gain, grad_out):
    length, width = mixer_input.shape
    heads = log_decay.shape[0]
    state_n = b_rows.shape[1]
    nc = ring
    q = length // nc
    kh = nc * heads
    pr = state_n // chips
    lb = width // 2 // LANES
    far = ring // 2
    vm = pltpu.VMEM
    piece = (lb, chips, pr, LANES)
    msg = (chips, lb * pr, LANES)
    msg_l = (chips, lb * pr + 8, LANES)
    scratch = [
        vm((nc, q, width), BF16), vm((nc, q, width), BF16),
        vm((nc, q, width), F32), vm((nc, q, width), F32),
        vm((nc, state_n, width), F32), vm((nc, state_n, width), F32),
        vm((nc, state_n, width), BF16), vm((nc, state_n, width), BF16),
        vm((nc, q, q), BF16), vm((nc, q, q), BF16),
        vm((nc, q, state_n), F32), vm((nc, q, state_n), F32),
        vm((nc, width), F32),
        vm((2 * kh, width), BF16), vm((q, 2 * kh), BF16), vm((q, 2 * kh), BF16),
        vm((2 * nc, width), F32), vm((1, width), F32), vm((3 * q, q), BF16), vm((1, width), F32),
        vm((state_n, width), F32), vm((state_n, width), F32),
        vm((2, *piece), F32), vm((2, *piece), F32), vm((2, 8, LANES), F32), vm((8, LANES), F32),
        vm(piece, F32), vm(piece, F32),
        vm(msg_l, F32), vm(msg, F32), vm(msg_l, F32), vm(msg, F32), vm(msg, F32), vm(msg, F32),
        vm(msg, F32), vm(msg, F32), vm(piece, F32), vm(piece, F32), vm(piece, F32), vm(piece, F32),
        vm((2, 2, far, q, state_n), F32),
        pltpu.SemaphoreType.DMA((5,)), pltpu.SemaphoreType.DMA((5,)),
        pltpu.SemaphoreType.DMA((4, chips)), pltpu.SemaphoreType.DMA((4, chips)),
        pltpu.SemaphoreType.DMA((2, 2, far)), pltpu.SemaphoreType.DMA((2, 2, far)),
    ]
    whole = pl.BlockSpec(memory_space=pltpu.VMEM)
    return pl.pallas_call(
        functools.partial(kernel, chips, ring),
        out_shape=(
            jax.ShapeDtypeStruct((length, width), BF16),
            jax.ShapeDtypeStruct((length, width), BF16),
            jax.ShapeDtypeStruct((heads, length), F32),
            jax.ShapeDtypeStruct((q, state_n), F32),
            jax.ShapeDtypeStruct((q, state_n), F32),
        ),
        in_specs=[whole] * 6,
        out_specs=(whole,) * 5,
        scratch_shapes=scratch,
        compiler_params=pltpu.CompilerParams(
            collective_id=0, has_side_effects=True, vmem_limit_bytes=60 * 1024 * 1024),
    )(mixer_input, log_decay, b_rows, c_rows, skip_gain.reshape(1, heads), grad_out)


def solution(mesh):
    chips = mesh.shape["seq"] // 2
    ring = mesh.shape["exp"]
    return jax.shard_map(
        functools.partial(body, chips, ring),
        mesh=mesh,
        in_specs=(
            P("seq", "exp"),
            P("exp", "seq"),
            P("seq", None),
            P("seq", None),
            P("exp"),
            P("seq", "exp"),
        ),
        out_specs=(
            P("seq", "exp"),
            P("seq", "exp"),
            P("exp", "seq"),
            P(("seq", "exp"), None),
            P(("seq", "exp"), None),
        ),
        check_vma=False,
    )
```

```python
import functools

import jax
import jax.numpy as jnp
from jax import lax
from jax.experimental import pallas as pl
from jax.experimental.pallas import tpu as pltpu
from jax.sharding import PartitionSpec as P

F32 = jnp.float32
BF16 = jnp.bfloat16
MESH = pl.DeviceIdType.MESH
HEAD = 64
LANES = 128


def dot(a, b, ca, cb):
    return lax.dot_general(a, b, (((ca,), (cb,)), ((), ())), preferred_element_type=F32)


def nn(a, b):
    return dot(a, b, 1, 0)


def nt(a, b):
    return dot(a, b, 1, 1)


def tn(a, b):
    return dot(a, b, 0, 0)


def iota(shape, axis):
    return lax.broadcasted_iota(jnp.int32, shape, axis)


def pieces(value, count, axis):
    out = []
    for _ in range(count):
        part = value.astype(BF16)
        value = value - part.astype(F32)
        out.append(part)
    return jnp.concatenate(out, axis=axis)


def kernel(chips, ring, x_ref, ld_ref, b_any, c_any, skip_ref, dy_ref,
           y_ref, dx_ref, gld_ref, gb_ref, gc_ref,
           xv, dyv, b_ref, c_ref, yv, dxv,
           xs, ds, a_exp, inv_exp, gmat, hmat, sp, tp, mm, mt, dcs, dbs, bnd,
           spread, parts_a, parts_i, rows, lam, tri_s, skipe,
           state, grad, th, tb, lamh, lamp, pf, pb, cmf, cmb, rf, rb, esf, esb,
           ref_, reb, p2f, p2b, pef, peb, rsbuf,
           in_s, out_s, lam_s, lam_r, pair_s, pair_r, a2a_s, a2a_r, rs_s, rs_r):
    seq = lax.axis_index("seq")
    z = lax.axis_index("exp")
    core = lax.rem(seq, 2)
    chip = seq // 2
    other = 1 - core
    partner = (chip * 2 + other, z)
    heads = ld_ref.shape[0]
    length, width = x_ref.shape
    nc = ring
    q = length // nc
    nx = min(4, chips)
    ny = chips // nx
    cx, cy = lax.rem(chip, nx), chip // nx
    state_n = b_ref.shape[1]
    pr = state_n // chips
    half = width // 2
    lb = half // LANES
    kh = nc * heads
    far = ring // 2

    def chip_dev(p):
        return (p * 2 + core, z)

    offsets = sorted(
        [(dy, dx) for dy in range(ny) for dx in range(nx) if (dy, dx) != (0, 0)],
        key=lambda o: (min(o[0], ny - o[0]) + min(o[1], nx - o[1]), o[0]))
    count = len(offsets)

    def chip_to(d):
        dy, dx = offsets[d]
        return lax.rem(cy + dy, ny) * nx + lax.rem(cx + dx, nx)

    def chip_from(d):
        dy, dx = offsets[d]
        return lax.rem(cy + ny - dy, ny) * nx + lax.rem(cx + nx - dx, nx)

    barrier = pltpu.get_barrier_semaphore()
    pl.semaphore_signal(barrier, inc=1, device_id=partner, device_id_type=MESH)
    for d in range(count):
        pl.semaphore_signal(barrier, inc=1, device_id=chip_dev(chip_to(d)), device_id_type=MESH)
    z_dn = lax.rem(z + ring - 1, ring)
    z_up = lax.rem(z + 1, ring)
    pl.semaphore_signal(barrier, inc=1, device_id=(seq, z_dn), device_id_type=MESH)
    pl.semaphore_signal(barrier, inc=1, device_id=(seq, z_up), device_id_type=MESH)

    def remote(src, dst, s_sem, r_sem, dev):
        return pltpu.make_async_remote_copy(
            src_ref=src, dst_ref=dst, send_sem=s_sem, recv_sem=r_sem,
            device_id=dev, device_id_type=MESH)

    def rows_of(c):
        return pl.ds(pl.multiple_of(c * q, q), q)

    def loads(k, src, dst, c):
        return pltpu.make_async_copy(src.at[rows_of(c)], dst.at[rows_of(c)], in_s.at[k, c])

    def whole_load(k):
        return pltpu.make_async_copy((b_any, c_any)[k], (b_ref, c_ref)[k], in_s.at[k, nc])

    whole_load(0).start()
    for c in range(nc):
        loads(0, x_ref, xv, c).start()
    whole_load(1).start()
    for c in reversed(range(nc)):
        loads(1, dy_ref, dyv, c).start()

    stacked = jnp.concatenate([ld_ref[:, c * q:(c + 1) * q] for c in range(nc)], axis=0)
    tri = (iota((q, q), 0) >= iota((q, q), 1)).astype(BF16)
    cum = nt(jnp.concatenate([tri] * 3, axis=1), pieces(stacked, 3, 1))
    tri_s[...] = jnp.concatenate([tri] * 3, axis=0)
    rho = cum[q // 2 - 1:q // 2, :]
    tot = cum[q - 1:q, :]
    shifted = cum - rho
    parts_a[...] = pieces(jnp.exp(shifted), 2, 1)
    parts_i[...] = pieces(jnp.exp(-shifted), 2, 1)
    one = (lax.rem(iota((kh, width), 0), heads) == iota((kh, width), 1) // HEAD).astype(BF16)
    spread[...] = jnp.concatenate([one, one], axis=0)
    own_row = iota((nc, kh), 1) // heads == iota((nc, kh), 0)
    pair_rows = jnp.concatenate(
        [jnp.where(own_row, jnp.exp(rho), 0.0), jnp.where(own_row, jnp.exp(tot - rho), 0.0)], axis=0)
    rows[...] = nn(pieces(pair_rows, 3, 1), jnp.concatenate([one, one, one], axis=0))
    both = rows[0:nc, :] * rows[nc:2 * nc, :]
    total = both[0:1, :]
    for c in range(1, nc):
        total = total * both[c:c + 1, :]
    lam[...] = total
    for h in range(2):
        for r in range(lb):
            lamh[h, r:r + 1, :] = total[:, h * half + r * LANES:h * half + (r + 1) * LANES]
    head_one = (iota((heads, width), 1) // HEAD == iota((heads, width), 0)).astype(BF16)
    skipe[...] = nn(pieces(skip_ref[...], 3, 1), jnp.concatenate([head_one] * 3, axis=0))

    lane_chunk = lax.rem(iota((q, 2 * kh), 1), kh) // heads

    state[...] = jnp.zeros_like(state)
    grad[...] = jnp.zeros_like(grad)

    def fwd_local(c, _):
        inv = nn(jnp.where(lane_chunk == c, parts_i[...], jnp.zeros((), BF16)), spread[...])
        inv_exp[c] = inv
        loads(0, x_ref, xv, c).wait()
        scaled = (xv[rows_of(c), :].astype(F32) * inv).astype(BF16)
        xs[c] = scaled
        got = tn(b_ref[rows_of(c), :], scaled)
        gmat[c] = got
        f = rows[pl.ds(c, 1), :]
        g = rows[pl.ds(nc + c, 1), :]
        state[...] = g * (f * state[...] + got)
        return 0

    def bwd_local(i, _):
        c = nc - 1 - i
        a = nn(jnp.where(lane_chunk == c, parts_a[...], jnp.zeros((), BF16)), spread[...])
        a_exp[c] = a
        loads(1, dy_ref, dyv, c).wait()
        scaled = (dyv[rows_of(c), :].astype(F32) * a).astype(BF16)
        ds[c] = scaled
        got = tn(c_ref[rows_of(c), :], scaled)
        hmat[c] = got
        f = rows[pl.ds(c, 1), :]
        g = rows[pl.ds(nc + c, 1), :]
        grad[...] = f * (g * grad[...] + got)
        return 0

    def to_halves(src, dst):
        for h in range(2):
            for r in range(lb):
                lo = h * half + r * LANES
                dst[h, :, r * pr:(r + 1) * pr, :] = src[:, lo:lo + LANES].reshape(chips, pr, LANES)

    first = core == 0

    def piece_of(d):
        return chip_to(d) if d < count else chip

    def pair_send(base, src, dst, which):
        out = []
        for d in range(count + 1):
            p = which(d)
            out.append(remote(src.at[p], dst.at[p], pair_s.at[base, d], pair_r.at[base, d], partner))
            out[-1].start()
        return out

    def pass_on(base, d, src, dst, p):
        copy = remote(src.at[p], dst.at[chip], a2a_s.at[base, d], a2a_r.at[base, d], chip_dev(p))
        copy.start()
        return copy

    def lam_rows():
        return ([lamh[core, r:r + 1, :] for r in range(lb)], [lamp[r:r + 1, :] for r in range(lb)])

    def combine(base, came, kept, got, out, dst, forward):
        lo_, lp_ = lam_rows()
        go = []
        for d in range(count + 1):
            p = piece_of(d)
            came[d].wait_recv()
            for r in range(lb):
                lanes = slice(r * pr, (r + 1) * pr)
                mine, theirs = kept[core, p, lanes, :], got[p, lanes, :]
                if forward:
                    value = jnp.where(first, lp_[r], 1.0) * mine + jnp.where(first, 1.0, lo_[r]) * theirs
                else:
                    value = jnp.where(first, 1.0, lp_[r]) * mine + jnp.where(first, lo_[r], 1.0) * theirs
                if d < count:
                    out[p, lanes, :] = value
                else:
                    dst[chip, lanes, :] = value
            if forward:
                for r in range(lb):
                    row = slice(lb * pr + r, lb * pr + r + 1)
                    if d < count:
                        out[p, row, :] = lo_[r] * lp_[r]
                    else:
                        dst[chip, row, :] = lo_[r] * lp_[r]
            if d < count:
                go.append(pass_on(base, d, out, dst, p))
        return go

    def scan_pieces(go, base, got, out, dst, order):
        for copy in go:
            copy.wait_recv()
        run = [jnp.zeros((pr, LANES), F32) for _ in range(lb)]
        for p in order:
            for r in range(lb):
                out[p, r * pr:(r + 1) * pr, :] = run[r]
                run[r] = rf[p, lb * pr + r:lb * pr + r + 1, :] * run[r] + got[p, r * pr:(r + 1) * pr, :]
        dst[chip] = out[chip]
        return [pass_on(base, d, out, dst, chip_to(d)) for d in range(count)]

    def place(dst, p, r, lane_half, value):
        lo = pl.multiple_of(lane_half * half + r * LANES, LANES)
        dst[pl.ds(pl.multiple_of(p * pr, pr), pr), pl.ds(lo, LANES)] = value

    def hand_out(base, ret, enters, kept, got, share, shared, dst, forward):
        lo_, lp_ = lam_rows()
        out = []
        for d in [count, *range(count)]:
            p = chip_from(d) if d < count else chip
            if d < count:
                ret[d].wait_recv()
            for r in range(lb):
                lanes = slice(r * pr, (r + 1) * pr)
                enter = enters[p, lanes, :]
                if forward:
                    past = jnp.where(first, lo_[r], lp_[r]) * enter + jnp.where(
                        first, kept[core, p, lanes, :], got[p, lanes, :])
                    own, theirs = jnp.where(first, enter, past), jnp.where(first, past, enter)
                else:
                    past = jnp.where(first, lp_[r], lo_[r]) * enter + jnp.where(
                        first, got[p, lanes, :], kept[core, p, lanes, :])
                    own, theirs = jnp.where(first, past, enter), jnp.where(first, enter, past)
                share[p, lanes, :] = theirs
                place(dst, p, r, core, own)
            copy = remote(share.at[p], shared.at[p], pair_s.at[base, d], pair_r.at[base, d], partner)
            copy.start()
            out.append((p, copy))
        return out

    def take_in(pairs, shared, dst):
        for p, copy in pairs:
            copy.wait_recv()
            for r in range(lb):
                place(dst, p, r, other, shared[p, r * pr:(r + 1) * pr, :])

    lower = iota((q, q), 0) >= iota((q, q), 1)
    upper = iota((q, q), 0) <= iota((q, q), 1)

    def inner(c, _):
        bb, cc = b_ref[rows_of(c), :], c_ref[rows_of(c), :]
        mm[c] = jnp.where(lower, nt(cc, bb), 0.0).astype(BF16)
        mt[c] = jnp.where(upper, nt(bb, cc), 0.0).astype(BF16)
        dm = jnp.where(lower, nt(ds[c], xs[c]), 0.0).astype(BF16)
        dcs[c] = nn(dm, bb)
        dbs[c] = tn(dm, cc)
        return 0

    whole_load(0).wait()
    lax.fori_loop(0, nc, fwd_local, 0)
    to_halves(state, th)
    pl.semaphore_wait(barrier, chips + 2)
    send_lam = remote(lamh.at[other], lamp, lam_s, lam_r, partner)
    send_lam.start()
    pair_f = pair_send(0, th.at[other], pf, piece_of)
    whole_load(1).wait()
    lax.fori_loop(0, nc // 2, bwd_local, 0)
    send_lam.wait_recv()
    go_f = combine(0, pair_f, th, pf, cmf, rf, True)
    lax.fori_loop(nc // 2, nc, bwd_local, 0)
    to_halves(grad, tb)
    pair_b = pair_send(1, tb.at[other], pb, piece_of)
    lax.fori_loop(0, nc // 4, inner, 0)
    go_b = combine(1, pair_b, tb, pb, cmb, rb, False)
    lax.fori_loop(nc // 4, nc // 2, inner, 0)
    ret_f = scan_pieces(go_f, 2, rf, esf, ref_, range(chips))
    lax.fori_loop(nc // 2, 3 * nc // 4, inner, 0)
    ret_b = scan_pieces(go_b, 3, rb, esb, reb, list(reversed(range(chips))))
    lax.fori_loop(3 * nc // 4, nc, inner, 0)
    send_2f = hand_out(2, ret_f, ref_, th, pf, p2f, pef, state, True)
    take_in(send_2f, pef, state)

    def fwd_state(c, _):
        f = rows[pl.ds(c, 1), :]
        g = rows[pl.ds(nc + c, 1), :]
        entering = f * state[...]
        sp[c] = entering.astype(BF16)
        leaving = entering + gmat[c]
        gmat[c] = leaving
        state[...] = g * leaving
        return 0

    lax.fori_loop(0, nc, fwd_state, 0)

    hq = q // 2

    def rs_copy(t, way, step, src):
        to = (seq, z_dn if way == 0 else z_up)
        dst = rsbuf.at[t, way, step]
        if step == 0:
            dst = dst.at[pl.ds(way * hq, hq)]
        return remote(src, dst, rs_s.at[t, way, step], rs_r.at[t, way, step], to)

    def chunk_at(way, step):
        gap = far - step
        return lax.rem(z + (ring - gap if way == 0 else gap), ring)

    started = {}

    def rs_start(t, own):
        for way in range(2):
            src = own.at[chunk_at(way, 0), pl.ds(way * hq, hq)]
            started[t, way, 0] = rs_copy(t, way, 0, src)
            started[t, way, 0].start()

    def rs_next(t, own, step):
        for way in range(2):
            started[t, way, step - 1].wait_recv()
            k = chunk_at(way, step)
            if step == 1:
                lo = way * hq
                rsbuf[t, way, 0, lo:lo + hq, :] += own[k, lo:lo + hq, :]
                lo = hq - lo
                rsbuf[t, way, 0, lo:lo + hq, :] = own[k, lo:lo + hq, :]
            else:
                rsbuf[t, way, step - 1] += own[k]
            started[t, way, step] = rs_copy(t, way, step, rsbuf.at[t, way, step - 1])
            started[t, way, step].start()

    def rs_end(t, own, out):
        for way in range(2):
            started[t, way, far - 1].wait_recv()
        last = rsbuf[t, 0, far - 1] + rsbuf[t, 1, far - 1]
        if far == 1:
            raise ValueError("ring")
        out[...] = own[z] + last

    def dc_chunk(i, _):
        c = lax.rem(z + far + i, ring)
        dcs[c] += nt(ds[c], sp[c])
        return 0

    def db_chunk(i, _):
        c = lax.rem(z + far + i, ring)
        dbs[c] += nt(xs[c], tp[c])
        return 0

    dc_chunk(0, 0)
    rs_start(0, dcs)
    lax.fori_loop(1, nc, dc_chunk, 0)

    send_2b = hand_out(3, ret_b, reb, tb, pb, p2b, peb, grad, False)
    take_in(send_2b, peb, grad)

    def bwd_state(i, _):
        c = nc - 1 - i
        f = rows[pl.ds(c, 1), :]
        g = rows[pl.ds(nc + c, 1), :]
        later = g * grad[...]
        low = later.astype(BF16)
        tp[c] = low
        bnd[pl.ds(c, 1), :] = jnp.sum(low.astype(F32) * gmat[c], axis=0, keepdims=True)
        grad[...] = f * (later + hmat[c])
        return 0

    lax.fori_loop(0, nc, bwd_state, 0)
    rs_next(0, dcs, 1)
    db_chunk(0, 0)
    rs_start(1, dbs)
    lax.fori_loop(1, nc, db_chunk, 0)

    last_row = iota((q, width), 0) == q - 1

    def stores(k, c):
        src, dst = ((yv, y_ref), (dxv, dx_ref))[k]
        return pltpu.make_async_copy(src.at[rows_of(c)], dst.at[rows_of(c)], out_s.at[k, c])

    def outputs(c, _):
        x_c, d_c = xs[c], ds[c]
        acc_y = nn(jnp.concatenate([mm[c], c_ref[rows_of(c), :]], axis=1),
                   jnp.concatenate([x_c, sp[c]], axis=0))
        acc_x = nn(jnp.concatenate([mt[c], b_ref[rows_of(c), :]], axis=1),
                   jnp.concatenate([d_c, tp[c]], axis=0))
        gain = skipe[...]
        yv[rows_of(c), :] = (a_exp[c] * acc_y + gain * xv[rows_of(c), :].astype(F32)).astype(BF16)
        dxv[rows_of(c), :] = (inv_exp[c] * acc_x + gain * dyv[rows_of(c), :].astype(F32)).astype(BF16)
        diff = d_c.astype(F32) * acc_y - x_c.astype(F32) * acc_x
        diff = diff + jnp.where(last_row, bnd[pl.ds(c, 1), :], 0.0)
        hi = diff.astype(BF16)
        lo = (diff - hi.astype(F32)).astype(BF16)
        per_head = nt(head_one, hi) + nt(head_one, lo)
        gld_ref[:, rows_of(c)] = nn(pieces(per_head, 3, 1), tri_s[...])
        stores(0, c).start()
        stores(1, c).start()
        return 0

    done = 0
    for step in range(1, far):
        upto = nc * step // far
        lax.fori_loop(done, upto, outputs, 0)
        done = upto
        if step + 1 < far:
            rs_next(0, dcs, step + 1)
        rs_next(1, dbs, step)
    lax.fori_loop(done, nc, outputs, 0)
    rs_end(0, dcs, gc_ref)
    rs_end(1, dbs, gb_ref)

    for c in range(nc):
        stores(0, c).wait()
        stores(1, c).wait()
    for copy in [send_lam, *pair_f, *pair_b, *go_f, *go_b, *ret_f, *ret_b,
                 *[c for _, c in send_2f], *[c for _, c in send_2b], *started.values()]:
        copy.wait_send()


def finish_kernel(*refs):
    count = (len(refs) - 1) // 2
    sems = refs[-1]
    copies = []
    for k in range(count):
        src, dst = refs[k], refs[count + k]
        parts = 4 if src.shape[0] >= 1024 else 1
        size = src.shape[0] // parts
        for i in range(parts):
            rows = pl.ds(i * size, size)
            copies.append(pltpu.make_async_copy(src.at[rows], dst.at[rows], sems.at[k, i]))
    for copy in copies:
        copy.start()
    for copy in copies:
        copy.wait()


def finish(arrays):
    anywhere = pl.BlockSpec(memory_space=pl.ANY)
    return pl.pallas_call(
        finish_kernel,
        out_shape=tuple(jax.ShapeDtypeStruct(a.shape, a.dtype) for a in arrays),
        in_specs=[anywhere] * len(arrays),
        out_specs=(anywhere,) * len(arrays),
        scratch_shapes=[pltpu.SemaphoreType.DMA((len(arrays), 4))],
    )(*arrays)


def body(chips, ring, mixer_input, log_decay, b_rows, c_rows, skip_gain, grad_out):
    length, width = mixer_input.shape
    heads = log_decay.shape[0]
    state_n = b_rows.shape[1]
    nc = ring
    q = length // nc
    kh = nc * heads
    pr = state_n // chips
    lb = width // 2 // LANES
    far = ring // 2
    vm = pltpu.VMEM
    msg = (chips, lb * pr, LANES)
    msg_l = (chips, lb * pr + 8, LANES)
    scratch = [
        vm((length, width), BF16), vm((length, width), BF16),
        vm((length, state_n), BF16), vm((length, state_n), BF16),
        vm((length, width), BF16), vm((length, width), BF16),
        vm((nc, q, width), BF16), vm((nc, q, width), BF16),
        vm((nc, q, width), F32), vm((nc, q, width), F32),
        vm((nc, state_n, width), F32), vm((nc, state_n, width), F32),
        vm((nc, state_n, width), BF16), vm((nc, state_n, width), BF16),
        vm((nc, q, q), BF16), vm((nc, q, q), BF16),
        vm((nc, q, state_n), F32), vm((nc, q, state_n), F32),
        vm((nc, width), F32),
        vm((2 * kh, width), BF16), vm((q, 2 * kh), BF16), vm((q, 2 * kh), BF16),
        vm((2 * nc, width), F32), vm((1, width), F32), vm((3 * q, q), BF16), vm((1, width), F32),
        vm((state_n, width), F32), vm((state_n, width), F32),
        vm((2, *msg), F32), vm((2, *msg), F32), vm((2, 8, LANES), F32), vm((8, LANES), F32),
        vm(msg, F32), vm(msg, F32),
        vm(msg_l, F32), vm(msg, F32), vm(msg_l, F32), vm(msg, F32), vm(msg, F32), vm(msg, F32),
        vm(msg, F32), vm(msg, F32), vm(msg, F32), vm(msg, F32), vm(msg, F32), vm(msg, F32),
        vm((2, 2, far, q, state_n), F32),
        pltpu.SemaphoreType.DMA((2, nc + 1)), pltpu.SemaphoreType.DMA((2, nc)),
        pltpu.SemaphoreType.DMA, pltpu.SemaphoreType.DMA,
        pltpu.SemaphoreType.DMA((4, chips)), pltpu.SemaphoreType.DMA((4, chips)),
        pltpu.SemaphoreType.DMA((4, chips)), pltpu.SemaphoreType.DMA((4, chips)),
        pltpu.SemaphoreType.DMA((2, 2, far)), pltpu.SemaphoreType.DMA((2, 2, far)),
    ]
    whole = pl.BlockSpec(memory_space=pltpu.VMEM)
    anywhere = pl.BlockSpec(memory_space=pl.ANY)
    return finish(pl.pallas_call(
        functools.partial(kernel, chips, ring),
        out_shape=(
            jax.ShapeDtypeStruct((length, width), BF16),
            jax.ShapeDtypeStruct((length, width), BF16),
            jax.ShapeDtypeStruct((heads, length), F32),
            jax.ShapeDtypeStruct((q, state_n), F32),
            jax.ShapeDtypeStruct((q, state_n), F32),
        ),
        in_specs=[anywhere, whole, anywhere, anywhere, whole, anywhere],
        out_specs=(anywhere, anywhere, whole, whole, whole),
        scratch_shapes=scratch,
        compiler_params=pltpu.CompilerParams(
            collective_id=0, has_side_effects=True, vmem_limit_bytes=60 * 1024 * 1024),
    )(mixer_input, log_decay, b_rows, c_rows, skip_gain.reshape(1, heads), grad_out))


def solution(mesh):
    chips = mesh.shape["seq"] // 2
    ring = mesh.shape["exp"]
    return jax.shard_map(
        functools.partial(body, chips, ring),
        mesh=mesh,
        in_specs=(
            P("seq", "exp"),
            P("exp", "seq"),
            P("seq", None),
            P("seq", None),
            P("exp"),
            P("seq", "exp"),
        ),
        out_specs=(
            P("seq", "exp"),
            P("seq", "exp"),
            P("exp", "seq"),
            P(("seq", "exp"), None),
            P(("seq", "exp"), None),
        ),
        check_vma=False,
    )
```

```python
import functools

import jax
import jax.numpy as jnp
from jax import lax
from jax.experimental import pallas as pl
from jax.experimental.pallas import tpu as pltpu
from jax.sharding import PartitionSpec as P

F32 = jnp.float32
BF16 = jnp.bfloat16
MESH = pl.DeviceIdType.MESH
HEAD = 64
LANES = 128


def dot(a, b, ca, cb):
    return lax.dot_general(a, b, (((ca,), (cb,)), ((), ())), preferred_element_type=F32)


def nn(a, b):
    return dot(a, b, 1, 0)


def nt(a, b):
    return dot(a, b, 1, 1)


def tn(a, b):
    return dot(a, b, 0, 0)


def iota(shape, axis):
    return lax.broadcasted_iota(jnp.int32, shape, axis)


def pieces(value, count, axis):
    out = []
    for _ in range(count):
        part = value.astype(BF16)
        value = value - part.astype(F32)
        out.append(part)
    return jnp.concatenate(out, axis=axis)


def kernel(chips, ring, x_ref, ld_any, b_any, c_any, skip_any, dy_ref,
           y_ref, dx_ref, gld_ref, gb_ref, gc_ref,
           xv, dyv, b_ref, c_ref, ld_ref, skip_ref,
           xs, ds, a_exp, inv_exp, gmat, hmat, sp, tp, mm, mt, dcs, dbs, bnd,
           spread, parts_a, parts_i, rows, lam, tri_s, skipe,
           state, grad, th, tb, lamh, lamp, pf, pb, cmf, cmb, rf, rb, esf, esb,
           ref_, reb, p2f, p2b, pef, peb, rsbuf,
           in_s, lam_s, lam_r, pair_s, pair_r, a2a_s, a2a_r, rs_s, rs_r):
    seq = lax.axis_index("seq")
    z = lax.axis_index("exp")
    core = lax.rem(seq, 2)
    chip = seq // 2
    other = 1 - core
    partner = (chip * 2 + other, z)
    heads = ld_ref.shape[0]
    length, width = x_ref.shape
    nc = ring
    q = length // nc
    nx = min(4, chips)
    ny = chips // nx
    cx, cy = lax.rem(chip, nx), chip // nx
    state_n = b_ref.shape[1]
    pr = state_n // chips
    half = width // 2
    lb = half // LANES
    kh = nc * heads
    far = ring // 2

    def chip_dev(p):
        return (p * 2 + core, z)

    offsets = sorted(
        [(dy, dx) for dy in range(ny) for dx in range(nx) if (dy, dx) != (0, 0)],
        key=lambda o: (min(o[0], ny - o[0]) + min(o[1], nx - o[1]), o[0]))
    count = len(offsets)

    def chip_to(d):
        dy, dx = offsets[d]
        return lax.rem(cy + dy, ny) * nx + lax.rem(cx + dx, nx)

    def chip_from(d):
        dy, dx = offsets[d]
        return lax.rem(cy + ny - dy, ny) * nx + lax.rem(cx + nx - dx, nx)

    barrier = pltpu.get_barrier_semaphore()
    pl.semaphore_signal(barrier, inc=1, device_id=partner, device_id_type=MESH)
    for d in range(count):
        pl.semaphore_signal(barrier, inc=1, device_id=chip_dev(chip_to(d)), device_id_type=MESH)
    z_dn = lax.rem(z + ring - 1, ring)
    z_up = lax.rem(z + 1, ring)
    pl.semaphore_signal(barrier, inc=1, device_id=(seq, z_dn), device_id_type=MESH)
    pl.semaphore_signal(barrier, inc=1, device_id=(seq, z_up), device_id_type=MESH)

    def remote(src, dst, s_sem, r_sem, dev):
        return pltpu.make_async_remote_copy(
            src_ref=src, dst_ref=dst, send_sem=s_sem, recv_sem=r_sem,
            device_id=dev, device_id_type=MESH)

    def rows_of(c):
        return pl.ds(pl.multiple_of(c * q, q), q)

    def loads(k, src, dst, c):
        return pltpu.make_async_copy(src.at[rows_of(c)], dst.at[rows_of(c)], in_s.at[k, c])

    def whole_load(k):
        src, dst = ((b_any, b_ref), (c_any, c_ref), (ld_any, ld_ref), (skip_any, skip_ref))[k]
        return pltpu.make_async_copy(src, dst, in_s.at[k % 2, nc + k // 2])

    for k in (2, 3, 0):
        whole_load(k).start()
    for c in range(nc):
        loads(0, x_ref, xv, c).start()
    whole_load(1).start()
    for c in reversed(range(nc)):
        loads(1, dy_ref, dyv, c).start()

    whole_load(2).wait()
    stacked = jnp.concatenate([ld_ref[:, c * q:(c + 1) * q] for c in range(nc)], axis=0)
    tri = (iota((q, q), 0) >= iota((q, q), 1)).astype(BF16)
    cum = nt(jnp.concatenate([tri] * 3, axis=1), pieces(stacked, 3, 1))
    tri_s[...] = jnp.concatenate([tri] * 3, axis=0)
    rho = cum[q // 2 - 1:q // 2, :]
    tot = cum[q - 1:q, :]
    shifted = cum - rho
    parts_a[...] = pieces(jnp.exp(shifted), 2, 1)
    parts_i[...] = pieces(jnp.exp(-shifted), 2, 1)
    one = (lax.rem(iota((kh, width), 0), heads) == iota((kh, width), 1) // HEAD).astype(BF16)
    spread[...] = jnp.concatenate([one, one], axis=0)
    own_row = iota((nc, kh), 1) // heads == iota((nc, kh), 0)
    pair_rows = jnp.concatenate(
        [jnp.where(own_row, jnp.exp(rho), 0.0), jnp.where(own_row, jnp.exp(tot - rho), 0.0)], axis=0)
    rows[...] = nn(pieces(pair_rows, 3, 1), jnp.concatenate([one, one, one], axis=0))
    both = rows[0:nc, :] * rows[nc:2 * nc, :]
    total = both[0:1, :]
    for c in range(1, nc):
        total = total * both[c:c + 1, :]
    lam[...] = total
    for h in range(2):
        for r in range(lb):
            lamh[h, r:r + 1, :] = total[:, h * half + r * LANES:h * half + (r + 1) * LANES]
    head_one = (iota((heads, width), 1) // HEAD == iota((heads, width), 0)).astype(BF16)
    whole_load(3).wait()
    skipe[...] = nn(pieces(skip_ref[...], 3, 1), jnp.concatenate([head_one] * 3, axis=0))

    lane_chunk = lax.rem(iota((q, 2 * kh), 1), kh) // heads

    state[...] = jnp.zeros_like(state)
    grad[...] = jnp.zeros_like(grad)

    def fwd_local(c, _):
        inv = nn(jnp.where(lane_chunk == c, parts_i[...], jnp.zeros((), BF16)), spread[...])
        inv_exp[c] = inv
        loads(0, x_ref, xv, c).wait()
        scaled = (xv[rows_of(c), :].astype(F32) * inv).astype(BF16)
        xs[c] = scaled
        got = tn(b_ref[rows_of(c), :], scaled)
        gmat[c] = got
        f = rows[pl.ds(c, 1), :]
        g = rows[pl.ds(nc + c, 1), :]
        state[...] = g * (f * state[...] + got)
        return 0

    def bwd_local(i, _):
        c = nc - 1 - i
        a = nn(jnp.where(lane_chunk == c, parts_a[...], jnp.zeros((), BF16)), spread[...])
        a_exp[c] = a
        loads(1, dy_ref, dyv, c).wait()
        scaled = (dyv[rows_of(c), :].astype(F32) * a).astype(BF16)
        ds[c] = scaled
        got = tn(c_ref[rows_of(c), :], scaled)
        hmat[c] = got
        f = rows[pl.ds(c, 1), :]
        g = rows[pl.ds(nc + c, 1), :]
        grad[...] = f * (g * grad[...] + got)
        return 0

    def to_halves(src, dst):
        for h in range(2):
            for r in range(lb):
                lo = h * half + r * LANES
                dst[h, :, r * pr:(r + 1) * pr, :] = src[:, lo:lo + LANES].reshape(chips, pr, LANES)

    first = core == 0

    def piece_of(d):
        return chip_to(d) if d < count else chip

    def pair_send(base, src, dst, which):
        out = []
        for d in range(count + 1):
            p = which(d)
            out.append(remote(src.at[p], dst.at[p], pair_s.at[base, d], pair_r.at[base, d], partner))
            out[-1].start()
        return out

    def pass_on(base, d, src, dst, p):
        copy = remote(src.at[p], dst.at[chip], a2a_s.at[base, d], a2a_r.at[base, d], chip_dev(p))
        copy.start()
        return copy

    def lam_rows():
        return ([lamh[core, r:r + 1, :] for r in range(lb)], [lamp[r:r + 1, :] for r in range(lb)])

    def combine(base, came, kept, got, out, dst, forward):
        lo_, lp_ = lam_rows()
        go = []
        for d in range(count + 1):
            p = piece_of(d)
            came[d].wait_recv()
            for r in range(lb):
                lanes = slice(r * pr, (r + 1) * pr)
                mine, theirs = kept[core, p, lanes, :], got[p, lanes, :]
                if forward:
                    value = jnp.where(first, lp_[r], 1.0) * mine + jnp.where(first, 1.0, lo_[r]) * theirs
                else:
                    value = jnp.where(first, 1.0, lp_[r]) * mine + jnp.where(first, lo_[r], 1.0) * theirs
                if d < count:
                    out[p, lanes, :] = value
                else:
                    dst[chip, lanes, :] = value
            if forward:
                for r in range(lb):
                    row = slice(lb * pr + r, lb * pr + r + 1)
                    if d < count:
                        out[p, row, :] = lo_[r] * lp_[r]
                    else:
                        dst[chip, row, :] = lo_[r] * lp_[r]
            if d < count:
                go.append(pass_on(base, d, out, dst, p))
        return go

    def scan_pieces(go, base, got, out, dst, order):
        for copy in go:
            copy.wait_recv()
        run = [jnp.zeros((pr, LANES), F32) for _ in range(lb)]
        for p in order:
            for r in range(lb):
                out[p, r * pr:(r + 1) * pr, :] = run[r]
                run[r] = rf[p, lb * pr + r:lb * pr + r + 1, :] * run[r] + got[p, r * pr:(r + 1) * pr, :]
        dst[chip] = out[chip]
        return [pass_on(base, d, out, dst, chip_to(d)) for d in range(count)]

    def place(dst, p, r, lane_half, value):
        lo = pl.multiple_of(lane_half * half + r * LANES, LANES)
        dst[pl.ds(pl.multiple_of(p * pr, pr), pr), pl.ds(lo, LANES)] = value

    def hand_out(base, ret, enters, kept, got, share, shared, dst, forward):
        lo_, lp_ = lam_rows()
        out = []
        for d in [count, *range(count)]:
            p = chip_from(d) if d < count else chip
            if d < count:
                ret[d].wait_recv()
            for r in range(lb):
                lanes = slice(r * pr, (r + 1) * pr)
                enter = enters[p, lanes, :]
                if forward:
                    past = jnp.where(first, lo_[r], lp_[r]) * enter + jnp.where(
                        first, kept[core, p, lanes, :], got[p, lanes, :])
                    own, theirs = jnp.where(first, enter, past), jnp.where(first, past, enter)
                else:
                    past = jnp.where(first, lp_[r], lo_[r]) * enter + jnp.where(
                        first, got[p, lanes, :], kept[core, p, lanes, :])
                    own, theirs = jnp.where(first, past, enter), jnp.where(first, enter, past)
                share[p, lanes, :] = theirs
                place(dst, p, r, core, own)
            copy = remote(share.at[p], shared.at[p], pair_s.at[base, d], pair_r.at[base, d], partner)
            copy.start()
            out.append((p, copy))
        return out

    def take_in(pairs, shared, dst):
        for p, copy in pairs:
            copy.wait_recv()
            for r in range(lb):
                place(dst, p, r, other, shared[p, r * pr:(r + 1) * pr, :])

    lower = iota((q, q), 0) >= iota((q, q), 1)
    upper = iota((q, q), 0) <= iota((q, q), 1)

    def inner(c, _):
        bb, cc = b_ref[rows_of(c), :], c_ref[rows_of(c), :]
        mm[c] = jnp.where(lower, nt(cc, bb), 0.0).astype(BF16)
        mt[c] = jnp.where(upper, nt(bb, cc), 0.0).astype(BF16)
        dm = jnp.where(lower, nt(ds[c], xs[c]), 0.0).astype(BF16)
        dcs[c] = nn(dm, bb)
        dbs[c] = tn(dm, cc)
        return 0

    whole_load(0).wait()
    lax.fori_loop(0, nc, fwd_local, 0)
    to_halves(state, th)
    pl.semaphore_wait(barrier, chips + 2)
    send_lam = remote(lamh.at[other], lamp, lam_s, lam_r, partner)
    send_lam.start()
    pair_f = pair_send(0, th.at[other], pf, piece_of)
    whole_load(1).wait()
    lax.fori_loop(0, nc // 2, bwd_local, 0)
    send_lam.wait_recv()
    go_f = combine(0, pair_f, th, pf, cmf, rf, True)
    lax.fori_loop(nc // 2, nc, bwd_local, 0)
    to_halves(grad, tb)
    pair_b = pair_send(1, tb.at[other], pb, piece_of)
    lax.fori_loop(0, nc // 4, inner, 0)
    go_b = combine(1, pair_b, tb, pb, cmb, rb, False)
    lax.fori_loop(nc // 4, nc // 2, inner, 0)
    ret_f = scan_pieces(go_f, 2, rf, esf, ref_, range(chips))
    lax.fori_loop(nc // 2, 3 * nc // 4, inner, 0)
    ret_b = scan_pieces(go_b, 3, rb, esb, reb, list(reversed(range(chips))))
    lax.fori_loop(3 * nc // 4, nc, inner, 0)
    send_2f = hand_out(2, ret_f, ref_, th, pf, p2f, pef, state, True)
    take_in(send_2f, pef, state)

    def fwd_state(c, _):
        f = rows[pl.ds(c, 1), :]
        g = rows[pl.ds(nc + c, 1), :]
        entering = f * state[...]
        sp[c] = entering.astype(BF16)
        leaving = entering + gmat[c]
        gmat[c] = leaving
        state[...] = g * leaving
        return 0

    lax.fori_loop(0, nc, fwd_state, 0)

    hq = q // 2

    def rs_copy(t, way, step, src):
        to = (seq, z_dn if way == 0 else z_up)
        dst = rsbuf.at[t, way, step]
        if step == 0:
            dst = dst.at[pl.ds(way * hq, hq)]
        return remote(src, dst, rs_s.at[t, way, step], rs_r.at[t, way, step], to)

    def chunk_at(way, step):
        gap = far - step
        return lax.rem(z + (ring - gap if way == 0 else gap), ring)

    started = {}

    def rs_start(t, own):
        for way in range(2):
            src = own.at[chunk_at(way, 0), pl.ds(way * hq, hq)]
            started[t, way, 0] = rs_copy(t, way, 0, src)
            started[t, way, 0].start()

    def rs_next(t, own, step):
        for way in range(2):
            started[t, way, step - 1].wait_recv()
            k = chunk_at(way, step)
            if step == 1:
                lo = way * hq
                rsbuf[t, way, 0, lo:lo + hq, :] += own[k, lo:lo + hq, :]
                lo = hq - lo
                rsbuf[t, way, 0, lo:lo + hq, :] = own[k, lo:lo + hq, :]
            else:
                rsbuf[t, way, step - 1] += own[k]
            started[t, way, step] = rs_copy(t, way, step, rsbuf.at[t, way, step - 1])
            started[t, way, step].start()

    def rs_end(t, own, out):
        for way in range(2):
            started[t, way, far - 1].wait_recv()
        last = rsbuf[t, 0, far - 1] + rsbuf[t, 1, far - 1]
        if far == 1:
            raise ValueError("ring")
        out[...] = own[z] + last

    def dc_chunk(i, _):
        c = lax.rem(z + far + i, ring)
        dcs[c] += nt(ds[c], sp[c])
        return 0

    def db_chunk(i, _):
        c = lax.rem(z + far + i, ring)
        dbs[c] += nt(xs[c], tp[c])
        return 0

    dc_chunk(0, 0)
    rs_start(0, dcs)
    lax.fori_loop(1, nc, dc_chunk, 0)

    send_2b = hand_out(3, ret_b, reb, tb, pb, p2b, peb, grad, False)
    take_in(send_2b, peb, grad)

    def bwd_state(i, _):
        c = nc - 1 - i
        f = rows[pl.ds(c, 1), :]
        g = rows[pl.ds(nc + c, 1), :]
        later = g * grad[...]
        low = later.astype(BF16)
        tp[c] = low
        bnd[pl.ds(c, 1), :] = jnp.sum(low.astype(F32) * gmat[c], axis=0, keepdims=True)
        grad[...] = f * (later + hmat[c])
        return 0

    lax.fori_loop(0, nc, bwd_state, 0)
    rs_next(0, dcs, 1)
    db_chunk(0, 0)
    rs_start(1, dbs)
    lax.fori_loop(1, nc, db_chunk, 0)

    last_row = iota((q, width), 0) == q - 1

    def outputs(c, _):
        x_c, d_c = xs[c], ds[c]
        acc_y = nn(jnp.concatenate([mm[c], c_ref[rows_of(c), :]], axis=1),
                   jnp.concatenate([x_c, sp[c]], axis=0))
        acc_x = nn(jnp.concatenate([mt[c], b_ref[rows_of(c), :]], axis=1),
                   jnp.concatenate([d_c, tp[c]], axis=0))
        gain = skipe[...]
        y_ref[rows_of(c), :] = (a_exp[c] * acc_y + gain * xv[rows_of(c), :].astype(F32)).astype(BF16)
        dx_ref[rows_of(c), :] = (inv_exp[c] * acc_x + gain * dyv[rows_of(c), :].astype(F32)).astype(BF16)
        diff = d_c.astype(F32) * acc_y - x_c.astype(F32) * acc_x
        diff = diff + jnp.where(last_row, bnd[pl.ds(c, 1), :], 0.0)
        hi = diff.astype(BF16)
        lo = (diff - hi.astype(F32)).astype(BF16)
        per_head = nt(head_one, hi) + nt(head_one, lo)
        gld_ref[:, rows_of(c)] = nn(pieces(per_head, 3, 1), tri_s[...])
        return 0

    done = 0
    for step in range(1, far):
        upto = nc * step // far
        lax.fori_loop(done, upto, outputs, 0)
        done = upto
        if step + 1 < far:
            rs_next(0, dcs, step + 1)
        rs_next(1, dbs, step)
    lax.fori_loop(done, nc, outputs, 0)
    rs_end(0, dcs, gc_ref)
    rs_end(1, dbs, gb_ref)

    for copy in [send_lam, *pair_f, *pair_b, *go_f, *go_b, *ret_f, *ret_b,
                 *[c for _, c in send_2f], *[c for _, c in send_2b], *started.values()]:
        copy.wait_send()


def finish_kernel(*refs):
    count = (len(refs) - 1) // 2
    sems = refs[-1]
    copies = []
    for k in range(count):
        src, dst = refs[k], refs[count + k]
        parts = 4 if src.shape[0] >= 1024 else 1
        size = src.shape[0] // parts
        for i in range(parts):
            rows = pl.ds(i * size, size)
            copies.append(pltpu.make_async_copy(src.at[rows], dst.at[rows], sems.at[k, i]))
    for copy in copies:
        copy.start()
    for copy in copies:
        copy.wait()


def finish(arrays):
    return pl.pallas_call(
        finish_kernel,
        out_shape=tuple(jax.ShapeDtypeStruct(a.shape, a.dtype) for a in arrays),
        in_specs=[pl.BlockSpec(memory_space=pltpu.VMEM)] * len(arrays),
        out_specs=(pl.BlockSpec(memory_space=pl.ANY),) * len(arrays),
        scratch_shapes=[pltpu.SemaphoreType.DMA((len(arrays), 4))],
        compiler_params=pltpu.CompilerParams(vmem_limit_bytes=16 * 1024 * 1024),
    )(*arrays)


def body(chips, ring, mixer_input, log_decay, b_rows, c_rows, skip_gain, grad_out):
    length, width = mixer_input.shape
    heads = log_decay.shape[0]
    state_n = b_rows.shape[1]
    nc = ring
    q = length // nc
    kh = nc * heads
    pr = state_n // chips
    lb = width // 2 // LANES
    far = ring // 2
    vm = pltpu.VMEM
    msg = (chips, lb * pr, LANES)
    msg_l = (chips, lb * pr + 8, LANES)
    scratch = [
        vm((length, width), BF16), vm((length, width), BF16),
        vm((length, state_n), BF16), vm((length, state_n), BF16),
        vm((heads, length), F32), vm((1, heads), F32),
        vm((nc, q, width), BF16), vm((nc, q, width), BF16),
        vm((nc, q, width), F32), vm((nc, q, width), F32),
        vm((nc, state_n, width), F32), vm((nc, state_n, width), F32),
        vm((nc, state_n, width), BF16), vm((nc, state_n, width), BF16),
        vm((nc, q, q), BF16), vm((nc, q, q), BF16),
        vm((nc, q, state_n), F32), vm((nc, q, state_n), F32),
        vm((nc, width), F32),
        vm((2 * kh, width), BF16), vm((q, 2 * kh), BF16), vm((q, 2 * kh), BF16),
        vm((2 * nc, width), F32), vm((1, width), F32), vm((3 * q, q), BF16), vm((1, width), F32),
        vm((state_n, width), F32), vm((state_n, width), F32),
        vm((2, *msg), F32), vm((2, *msg), F32), vm((2, 8, LANES), F32), vm((8, LANES), F32),
        vm(msg, F32), vm(msg, F32),
        vm(msg_l, F32), vm(msg, F32), vm(msg_l, F32), vm(msg, F32), vm(msg, F32), vm(msg, F32),
        vm(msg, F32), vm(msg, F32), vm(msg, F32), vm(msg, F32), vm(msg, F32), vm(msg, F32),
        vm((2, 2, far, q, state_n), F32),
        pltpu.SemaphoreType.DMA((2, nc + 2)),
        pltpu.SemaphoreType.DMA, pltpu.SemaphoreType.DMA,
        pltpu.SemaphoreType.DMA((4, chips)), pltpu.SemaphoreType.DMA((4, chips)),
        pltpu.SemaphoreType.DMA((4, chips)), pltpu.SemaphoreType.DMA((4, chips)),
        pltpu.SemaphoreType.DMA((2, 2, far)), pltpu.SemaphoreType.DMA((2, 2, far)),
    ]
    whole = pl.BlockSpec(memory_space=pltpu.VMEM)
    outside = pl.BlockSpec(memory_space=pltpu.HBM)
    return finish(pl.pallas_call(
        functools.partial(kernel, chips, ring),
        out_shape=(
            vm((length, width), BF16),
            vm((length, width), BF16),
            vm((heads, length), F32),
            vm((q, state_n), F32),
            vm((q, state_n), F32),
        ),
        in_specs=[outside] * 6,
        out_specs=(whole,) * 5,
        scratch_shapes=scratch,
        compiler_params=pltpu.CompilerParams(
            collective_id=0, has_side_effects=True, vmem_limit_bytes=48 * 1024 * 1024),
    )(*[pltpu.with_memory_space_constraint(a, pltpu.HBM) for a in (
        mixer_input, log_decay, b_rows, c_rows, skip_gain.reshape(1, heads), grad_out)]))


def solution(mesh):
    chips = mesh.shape["seq"] // 2
    ring = mesh.shape["exp"]
    return jax.shard_map(
        functools.partial(body, chips, ring),
        mesh=mesh,
        in_specs=(
            P("seq", "exp"),
            P("exp", "seq"),
            P("seq", None),
            P("seq", None),
            P("exp"),
            P("seq", "exp"),
        ),
        out_specs=(
            P("seq", "exp"),
            P("seq", "exp"),
            P("exp", "seq"),
            P(("seq", "exp"), None),
            P(("seq", "exp"), None),
        ),
        check_vma=False,
    )
```

```python
import functools

import jax
import jax.numpy as jnp
from jax import lax
from jax.experimental import pallas as pl
from jax.experimental.pallas import tpu as pltpu
from jax.sharding import PartitionSpec as P

F32 = jnp.float32
BF16 = jnp.bfloat16
MESH = pl.DeviceIdType.MESH
HEAD = 64
LANES = 128


def dot(a, b, ca, cb):
    return lax.dot_general(a, b, (((ca,), (cb,)), ((), ())), preferred_element_type=F32)


def nn(a, b):
    return dot(a, b, 1, 0)


def nt(a, b):
    return dot(a, b, 1, 1)


def tn(a, b):
    return dot(a, b, 0, 0)


def iota(shape, axis):
    return lax.broadcasted_iota(jnp.int32, shape, axis)


def pieces(value, count, axis):
    out = []
    for _ in range(count):
        part = value.astype(BF16)
        value = value - part.astype(F32)
        out.append(part)
    return jnp.concatenate(out, axis=axis)


def kernel(chips, ring, x_ref, ld_any, b_any, c_any, skip_any, dy_ref,
           y_ref, dx_ref, gld_ref, gb_ref, gc_ref,
           xv, dyv, b_ref, c_ref, ld_ref, skip_ref,
           xs, ds, a_exp, inv_exp, gmat, hmat, sp, tp, mm, mt, dcs, dbs, bnd,
           spread, parts_a, parts_i, rows, heads_of, tri_s, skipe,
           state, grad, th, tb, lamh, lamp, pf, pb, cmf, cmb, rf, rb, esf, esb,
           ref_, reb, p2f, p2b, pef, peb, rsbuf,
           in_s, lam_s, lam_r, pair_s, pair_r, a2a_s, a2a_r, rs_s, rs_r):
    seq = lax.axis_index("seq")
    z = lax.axis_index("exp")
    core = lax.rem(seq, 2)
    chip = seq // 2
    other = 1 - core
    partner = (chip * 2 + other, z)
    heads = ld_ref.shape[0]
    length, width = x_ref.shape
    nc = ring
    q = length // nc
    nx = min(4, chips)
    ny = chips // nx
    cx, cy = lax.rem(chip, nx), chip // nx
    state_n = b_ref.shape[1]
    pr = state_n // chips
    half = width // 2
    lb = half // LANES
    kh = nc * heads
    far = ring // 2

    def chip_dev(p):
        return (p * 2 + core, z)

    offsets = sorted(
        [(dy, dx) for dy in range(ny) for dx in range(nx) if (dy, dx) != (0, 0)],
        key=lambda o: (min(o[0], ny - o[0]) + min(o[1], nx - o[1]), o[0]))
    count = len(offsets)

    def chip_to(d):
        dy, dx = offsets[d]
        return lax.rem(cy + dy, ny) * nx + lax.rem(cx + dx, nx)

    def chip_from(d):
        dy, dx = offsets[d]
        return lax.rem(cy + ny - dy, ny) * nx + lax.rem(cx + nx - dx, nx)

    def remote(src, dst, s_sem, r_sem, dev):
        return pltpu.make_async_remote_copy(
            src_ref=src, dst_ref=dst, send_sem=s_sem, recv_sem=r_sem,
            device_id=dev, device_id_type=MESH)

    def rows_of(c):
        return pl.ds(pl.multiple_of(c * q, q), q)

    quart = length // 4

    def loads(k, part):
        src, dst = ((x_ref, xv), (dy_ref, dyv))[k]
        span = pl.ds(part * quart, quart)
        return pltpu.make_async_copy(src.at[span], dst.at[span], in_s.at[k, part])

    def whole_load(k):
        src, dst = ((b_any, b_ref), (c_any, c_ref), (ld_any, ld_ref), (skip_any, skip_ref))[k]
        return pltpu.make_async_copy(src, dst, in_s.at[k % 2, 4 + k // 2])

    whole_load(2).start()
    for part in range(4):
        loads(0, part).start()
    for k in (0, 1, 3):
        whole_load(k).start()
    for part in range(4):
        loads(1, part).start()

    barrier = pltpu.get_barrier_semaphore()
    pl.semaphore_signal(barrier, inc=1, device_id=partner, device_id_type=MESH)
    for d in range(count):
        pl.semaphore_signal(barrier, inc=1, device_id=chip_dev(chip_to(d)), device_id_type=MESH)
    z_dn = lax.rem(z + ring - 1, ring)
    z_up = lax.rem(z + 1, ring)
    pl.semaphore_signal(barrier, inc=1, device_id=(seq, z_dn), device_id_type=MESH)
    pl.semaphore_signal(barrier, inc=1, device_id=(seq, z_up), device_id_type=MESH)

    def head_of(shape, axis):
        return lax.shift_right_logical(iota(shape, axis), HEAD.bit_length() - 1)

    lane_heads = heads.bit_length() - 1
    one = ((iota((kh, width), 0) & (heads - 1)) == head_of((kh, width), 1)).astype(BF16)
    spread[0:kh, :] = one
    spread[kh:2 * kh, :] = one
    tri = (iota((q, q), 0) >= iota((q, q), 1)).astype(BF16)
    tri3 = jnp.concatenate([tri] * 3, axis=1)
    own_row = lax.shift_right_logical(iota((nc, kh), 1), lane_heads) == iota((nc, kh), 0)
    lane_chunk = lax.shift_right_logical(iota((q, 2 * kh), 1) & (kh - 1), lane_heads)

    whole_load(2).wait()
    stacked = jnp.concatenate([ld_ref[:, c * q:(c + 1) * q] for c in range(nc)], axis=0)
    cum = nt(tri3, pieces(stacked, 3, 1))
    rho = cum[q // 2 - 1:q // 2, :]
    tot = cum[q - 1:q, :]
    shifted = cum - rho
    parts_i[...] = pieces(jnp.exp(-shifted), 2, 1)
    parts_a[...] = pieces(jnp.exp(shifted), 2, 1)

    def by_chunk(parts):
        return jnp.concatenate(
            [jnp.where(lane_chunk == c, parts[...], jnp.zeros((), BF16)) for c in range(nc)], axis=0)

    inv_exp[...] = nn(by_chunk(parts_i), spread[...])
    pair_rows = jnp.concatenate(
        [jnp.where(own_row, jnp.exp(rho), 0.0), jnp.where(own_row, jnp.exp(tot - rho), 0.0)], axis=0)
    rows[...] = nn(pieces(pair_rows, 3, 1), jnp.concatenate([one, one, one], axis=0))
    both = rows[0:nc, :] * rows[nc:2 * nc, :]
    total = both[0:1, :]
    for c in range(1, nc):
        total = total * both[c:c + 1, :]
    for h in range(2):
        for r in range(lb):
            lamh[h, r:r + 1, :] = total[:, h * half + r * LANES:h * half + (r + 1) * LANES]

    def fwd_local(c):
        if c % (nc // 4) == 0:
            loads(0, c // (nc // 4)).wait()
        rc = slice(c * q, (c + 1) * q)
        scaled = (xv[rc, :].astype(F32) * inv_exp[rc, :]).astype(BF16)
        xs[c] = scaled
        got = tn(b_ref[rc, :], scaled)
        gmat[c] = got
        f = rows[c:c + 1, :]
        g = rows[nc + c:nc + c + 1, :]
        state[...] = g * got if c == 0 else g * (f * state[...] + got)

    def bwd_local(c):
        if (c + 1) % (nc // 4) == 0:
            loads(1, c // (nc // 4)).wait()
        rc = slice(c * q, (c + 1) * q)
        scaled = (dyv[rc, :].astype(F32) * a_exp[rc, :]).astype(BF16)
        ds[c] = scaled
        got = tn(c_ref[rc, :], scaled)
        hmat[c] = got
        f = rows[c:c + 1, :]
        g = rows[nc + c:nc + c + 1, :]
        grad[...] = f * got if c == nc - 1 else f * (g * grad[...] + got)

    def to_halves(src, dst):
        for h in range(2):
            for r in range(lb):
                lo = h * half + r * LANES
                dst[h, :, r * pr:(r + 1) * pr, :] = src[:, lo:lo + LANES].reshape(chips, pr, LANES)

    first = core == 0

    def piece_of(d):
        return chip_to(d) if d < count else chip

    def pair_send(base, src, dst, which):
        out = []
        for d in range(count + 1):
            p = which(d)
            out.append(remote(src.at[p], dst.at[p], pair_s.at[base, d], pair_r.at[base, d], partner))
            out[-1].start()
        return out

    def pass_on(base, d, src, dst, p):
        copy = remote(src.at[p], dst.at[chip], a2a_s.at[base, d], a2a_r.at[base, d], chip_dev(p))
        copy.start()
        return copy

    def lam_rows():
        return ([lamh[core, r:r + 1, :] for r in range(lb)], [lamp[r:r + 1, :] for r in range(lb)])

    def combine(base, came, kept, got, out, dst, forward):
        lo_, lp_ = lam_rows()
        go = []
        for d in range(count + 1):
            p = piece_of(d)
            came[d].wait_recv()
            for r in range(lb):
                lanes = slice(r * pr, (r + 1) * pr)
                mine, theirs = kept[core, p, lanes, :], got[p, lanes, :]
                if forward:
                    value = jnp.where(first, lp_[r], 1.0) * mine + jnp.where(first, 1.0, lo_[r]) * theirs
                else:
                    value = jnp.where(first, 1.0, lp_[r]) * mine + jnp.where(first, lo_[r], 1.0) * theirs
                if d < count:
                    out[p, lanes, :] = value
                else:
                    dst[chip, lanes, :] = value
            if forward:
                for r in range(lb):
                    row = slice(lb * pr + r, lb * pr + r + 1)
                    if d < count:
                        out[p, row, :] = lo_[r] * lp_[r]
                    else:
                        dst[chip, row, :] = lo_[r] * lp_[r]
            if d < count:
                go.append(pass_on(base, d, out, dst, p))
        return go

    def scan_pieces(go, base, got, out, dst, order):
        for copy in go:
            copy.wait_recv()
        run = [jnp.zeros((pr, LANES), F32) for _ in range(lb)]
        for p in order:
            for r in range(lb):
                out[p, r * pr:(r + 1) * pr, :] = run[r]
                run[r] = rf[p, lb * pr + r:lb * pr + r + 1, :] * run[r] + got[p, r * pr:(r + 1) * pr, :]
        dst[chip] = out[chip]
        return [pass_on(base, d, out, dst, chip_to(d)) for d in range(count)]

    def place(dst, p, r, lane_half, value):
        lo = pl.multiple_of(lane_half * half + r * LANES, LANES)
        dst[pl.ds(pl.multiple_of(p * pr, pr), pr), pl.ds(lo, LANES)] = value

    def hand_out(base, ret, enters, kept, got, share, shared, dst, forward):
        lo_, lp_ = lam_rows()
        out = []
        for d in [count, *range(count)]:
            p = chip_from(d) if d < count else chip
            if d < count:
                ret[d].wait_recv()
            for r in range(lb):
                lanes = slice(r * pr, (r + 1) * pr)
                enter = enters[p, lanes, :]
                if forward:
                    past = jnp.where(first, lo_[r], lp_[r]) * enter + jnp.where(
                        first, kept[core, p, lanes, :], got[p, lanes, :])
                    own, theirs = jnp.where(first, enter, past), jnp.where(first, past, enter)
                else:
                    past = jnp.where(first, lp_[r], lo_[r]) * enter + jnp.where(
                        first, got[p, lanes, :], kept[core, p, lanes, :])
                    own, theirs = jnp.where(first, past, enter), jnp.where(first, enter, past)
                share[p, lanes, :] = theirs
                place(dst, p, r, core, own)
            copy = remote(share.at[p], shared.at[p], pair_s.at[base, d], pair_r.at[base, d], partner)
            copy.start()
            out.append((p, copy))
        return out

    def take_in(pairs, shared, dst):
        for p, copy in pairs:
            copy.wait_recv()
            for r in range(lb):
                place(dst, p, r, other, shared[p, r * pr:(r + 1) * pr, :])

    lower = iota((q, q), 0) >= iota((q, q), 1)
    upper = iota((q, q), 0) <= iota((q, q), 1)

    def inner(c):
        rc = slice(c * q, (c + 1) * q)
        bb, cc = b_ref[rc, :], c_ref[rc, :]
        mm[c] = jnp.where(lower, nt(cc, bb), 0.0).astype(BF16)
        mt[c] = jnp.where(upper, nt(bb, cc), 0.0).astype(BF16)
        dm = jnp.where(lower, nt(ds[c], xs[c]), 0.0).astype(BF16)
        dcs[c] = nn(dm, bb)
        dbs[c] = tn(dm, cc)

    whole_load(0).wait()
    for c in range(nc):
        fwd_local(c)
    to_halves(state, th)
    pl.semaphore_wait(barrier, chips + 2)
    send_lam = remote(lamh.at[other], lamp, lam_s, lam_r, partner)
    send_lam.start()
    pair_f = pair_send(0, th.at[other], pf, piece_of)
    whole_load(1).wait()
    a_exp[...] = nn(by_chunk(parts_a), spread[...])
    for c in reversed(range(nc // 2, nc)):
        bwd_local(c)
    send_lam.wait_recv()
    go_f = combine(0, pair_f, th, pf, cmf, rf, True)
    for c in reversed(range(nc // 2)):
        bwd_local(c)
    to_halves(grad, tb)
    pair_b = pair_send(1, tb.at[other], pb, piece_of)
    whole_load(3).wait()
    for c in range(nc // 4):
        inner(c)
    go_b = combine(1, pair_b, tb, pb, cmb, rb, False)
    for c in range(nc // 4, nc // 2):
        inner(c)
    ret_f = scan_pieces(go_f, 2, rf, esf, ref_, range(chips))
    for c in range(nc // 2, 3 * nc // 4):
        inner(c)
    ret_b = scan_pieces(go_b, 3, rb, esb, reb, list(reversed(range(chips))))
    for c in range(3 * nc // 4, nc):
        inner(c)
    tri_s[...] = jnp.concatenate([tri] * 3, axis=0)
    head_one = (head_of((heads, width), 1) == iota((heads, width), 0)).astype(BF16)
    skipe[...] = nn(pieces(skip_ref[...], 3, 1), jnp.concatenate([head_one] * 3, axis=0))
    col = (head_of((width, heads), 0) == iota((width, heads), 1)).astype(BF16)
    heads_of[...] = jnp.concatenate([col, col], axis=0)
    send_2f = hand_out(2, ret_f, ref_, th, pf, p2f, pef, state, True)
    take_in(send_2f, pef, state)

    for c in range(nc):
        entering = rows[c:c + 1, :] * state[...]
        sp[c] = entering.astype(BF16)
        leaving = entering + gmat[c]
        gmat[c] = leaving
        state[...] = rows[nc + c:nc + c + 1, :] * leaving

    hq = q // 2
    started = {}

    def chunk_at(way, step):
        gap = far - step
        return lax.rem(z + (ring - gap if way == 0 else gap), ring)

    def rs_send(t, own, way, step, long):
        lo = (way if long else 1 - way) * hq
        first_step = 0 if long else 1
        k = chunk_at(way, step)
        if step == first_step:
            src = own.at[k, pl.ds(lo, hq)]
        else:
            started[t, way, step - 1, long].wait_recv()
            rsbuf[t, way, step - 1, lo:lo + hq, :] += own[k, lo:lo + hq, :]
            src = rsbuf.at[t, way, step - 1, pl.ds(lo, hq)]
        copy = remote(src, rsbuf.at[t, way, step, pl.ds(lo, hq)],
                      rs_s.at[t, way, step, int(long)], rs_r.at[t, way, step, int(long)],
                      (seq, z_dn if way == 0 else z_up))
        copy.start()
        started[t, way, step, long] = copy

    def rs_poll(t, own, step):
        for way in range(2):
            rs_send(t, own, way, step, True)
        if step + 1 < far:
            for way in range(2):
                rs_send(t, own, way, step + 1, False)

    def rs_end(t, own, out):
        for way in range(2):
            for long in (False, True):
                started[t, way, far - 1, long].wait_recv()
        out[...] = own[z] + rsbuf[t, 0, far - 1] + rsbuf[t, 1, far - 1]

    def near(i):
        gap = far - (i + 1) // 2
        return lax.rem(z + (gap if i % 2 == 1 else ring - gap), ring)

    def dc_chunk(i):
        c = near(i)
        dcs[c] += nt(ds[c], sp[c])

    def db_chunk(i):
        c = near(i)
        dbs[c] += nt(xs[c], tp[c])

    for i in range(3):
        dc_chunk(i)
    rs_poll(0, dcs, 0)
    send_2b = hand_out(3, ret_b, reb, tb, pb, p2b, peb, grad, False)
    for i in range(3, nc):
        dc_chunk(i)
    rs_poll(0, dcs, 1)
    take_in(send_2b, peb, grad)

    for c in reversed(range(nc)):
        later = rows[nc + c:nc + c + 1, :] * grad[...]
        low = later.astype(BF16)
        tp[c] = low
        bnd[c:c + 1, :] = jnp.sum(low.astype(F32) * gmat[c], axis=0, keepdims=True)
        if c:
            grad[...] = rows[c:c + 1, :] * (later + hmat[c])
    for i in range(3):
        db_chunk(i)
    rs_poll(1, dbs, 0)
    rs_poll(0, dcs, 2) if far > 2 else None
    for i in range(3, nc):
        db_chunk(i)

    last_row = iota((q, width), 0) == q - 1

    def outputs(c):
        rc = slice(c * q, (c + 1) * q)
        x_c, d_c = xs[c], ds[c]
        acc_y = nn(jnp.concatenate([mm[c], c_ref[rc, :]], axis=1),
                   jnp.concatenate([x_c, sp[c]], axis=0))
        acc_x = nn(jnp.concatenate([mt[c], b_ref[rc, :]], axis=1),
                   jnp.concatenate([d_c, tp[c]], axis=0))
        gain = skipe[...]
        y_ref[rc, :] = (a_exp[rc, :] * acc_y + gain * xv[rc, :].astype(F32)).astype(BF16)
        dx_ref[rc, :] = (inv_exp[rc, :] * acc_x + gain * dyv[rc, :].astype(F32)).astype(BF16)
        diff = d_c.astype(F32) * acc_y - x_c.astype(F32) * acc_x
        diff = diff + jnp.where(last_row, bnd[c:c + 1, :], 0.0)
        per_head = nn(pieces(diff, 2, 1), heads_of[...])
        gld_ref[:, rc] = tn(pieces(per_head, 3, 0), tri_s[...])

    done = 0
    for step in range(1, far):
        upto = nc * step // far
        for c in range(done, upto):
            outputs(c)
        done = upto
        if 2 < step + 2 < far:
            rs_poll(0, dcs, step + 2)
        rs_poll(1, dbs, step)
    for c in range(done, nc):
        outputs(c)
    rs_end(0, dcs, gc_ref)
    rs_end(1, dbs, gb_ref)
    for copy in [send_lam, *pair_f, *pair_b, *go_f, *go_b, *ret_f, *ret_b,
                 *[c for _, c in send_2f], *[c for _, c in send_2b], *started.values()]:
        copy.wait_send()


def finish_kernel(*refs):
    count = (len(refs) - 1) // 2
    sems = refs[-1]
    copies = []
    for k in range(count):
        src, dst = refs[k], refs[count + k]
        parts = 4 if src.shape[0] >= 1024 else 1
        size = src.shape[0] // parts
        for i in range(parts):
            rows = pl.ds(i * size, size)
            copies.append(pltpu.make_async_copy(src.at[rows], dst.at[rows], sems.at[k, i]))
    for copy in copies:
        copy.start()
    for copy in copies:
        copy.wait()


def finish(arrays):
    return pl.pallas_call(
        finish_kernel,
        out_shape=tuple(jax.ShapeDtypeStruct(a.shape, a.dtype) for a in arrays),
        in_specs=[pl.BlockSpec(memory_space=pltpu.VMEM)] * len(arrays),
        out_specs=(pl.BlockSpec(memory_space=pl.ANY),) * len(arrays),
        scratch_shapes=[pltpu.SemaphoreType.DMA((len(arrays), 4))],
        compiler_params=pltpu.CompilerParams(vmem_limit_bytes=16 * 1024 * 1024),
    )(*arrays)


def body(chips, ring, mixer_input, log_decay, b_rows, c_rows, skip_gain, grad_out):
    length, width = mixer_input.shape
    heads = log_decay.shape[0]
    state_n = b_rows.shape[1]
    nc = ring
    q = length // nc
    kh = nc * heads
    pr = state_n // chips
    lb = width // 2 // LANES
    far = ring // 2
    vm = pltpu.VMEM
    msg = (chips, lb * pr, LANES)
    msg_l = (chips, lb * pr + 8, LANES)
    scratch = [
        vm((length, width), BF16), vm((length, width), BF16),
        vm((length, state_n), BF16), vm((length, state_n), BF16),
        vm((heads, length), F32), vm((1, heads), F32),
        vm((nc, q, width), BF16), vm((nc, q, width), BF16),
        vm((length, width), F32), vm((length, width), F32),
        vm((nc, state_n, width), F32), vm((nc, state_n, width), F32),
        vm((nc, state_n, width), BF16), vm((nc, state_n, width), BF16),
        vm((nc, q, q), BF16), vm((nc, q, q), BF16),
        vm((nc, q, state_n), F32), vm((nc, q, state_n), F32),
        vm((nc, width), F32),
        vm((2 * kh, width), BF16), vm((q, 2 * kh), BF16), vm((q, 2 * kh), BF16),
        vm((2 * nc, width), F32), vm((2 * width, heads), BF16), vm((3 * q, q), BF16), vm((1, width), F32),
        vm((state_n, width), F32), vm((state_n, width), F32),
        vm((2, *msg), F32), vm((2, *msg), F32), vm((2, 8, LANES), F32), vm((8, LANES), F32),
        vm(msg, F32), vm(msg, F32),
        vm(msg_l, F32), vm(msg, F32), vm(msg_l, F32), vm(msg, F32), vm(msg, F32), vm(msg, F32),
        vm(msg, F32), vm(msg, F32), vm(msg, F32), vm(msg, F32), vm(msg, F32), vm(msg, F32),
        vm((2, 2, far, q, state_n), F32),
        pltpu.SemaphoreType.DMA((2, 6)),
        pltpu.SemaphoreType.DMA, pltpu.SemaphoreType.DMA,
        pltpu.SemaphoreType.DMA((4, chips)), pltpu.SemaphoreType.DMA((4, chips)),
        pltpu.SemaphoreType.DMA((4, chips)), pltpu.SemaphoreType.DMA((4, chips)),
        pltpu.SemaphoreType.DMA((2, 2, far, 2)), pltpu.SemaphoreType.DMA((2, 2, far, 2)),
    ]
    whole = pl.BlockSpec(memory_space=pltpu.VMEM)
    outside = pl.BlockSpec(memory_space=pltpu.HBM)
    return finish(pl.pallas_call(
        functools.partial(kernel, chips, ring),
        out_shape=(
            vm((length, width), BF16),
            vm((length, width), BF16),
            vm((heads, length), F32),
            vm((q, state_n), F32),
            vm((q, state_n), F32),
        ),
        in_specs=[outside] * 6,
        out_specs=(whole,) * 5,
        scratch_shapes=scratch,
        compiler_params=pltpu.CompilerParams(
            collective_id=0, has_side_effects=True, vmem_limit_bytes=48 * 1024 * 1024),
    )(*[pltpu.with_memory_space_constraint(a, pltpu.HBM) for a in (
        mixer_input, log_decay, b_rows, c_rows, skip_gain.reshape(1, heads), grad_out)]))


def solution(mesh):
    chips = mesh.shape["seq"] // 2
    ring = mesh.shape["exp"]
    return jax.shard_map(
        functools.partial(body, chips, ring),
        mesh=mesh,
        in_specs=(
            P("seq", "exp"),
            P("exp", "seq"),
            P("seq", None),
            P("seq", None),
            P("exp"),
            P("seq", "exp"),
        ),
        out_specs=(
            P("seq", "exp"),
            P("seq", "exp"),
            P("exp", "seq"),
            P(("seq", "exp"), None),
            P(("seq", "exp"), None),
        ),
        check_vma=False,
    )
```

```python
import functools

import jax
import jax.numpy as jnp
from jax import lax
from jax.experimental import pallas as pl
from jax.experimental.pallas import tpu as pltpu
from jax.sharding import PartitionSpec as P

F32 = jnp.float32
BF16 = jnp.bfloat16
MESH = pl.DeviceIdType.MESH
HEAD = 64
LANES = 128


def dot(a, b, ca, cb):
    return lax.dot_general(a, b, (((ca,), (cb,)), ((), ())), preferred_element_type=F32)


def nn(a, b):
    return dot(a, b, 1, 0)


def nt(a, b):
    return dot(a, b, 1, 1)


def tn(a, b):
    return dot(a, b, 0, 0)


def iota(shape, axis):
    return lax.broadcasted_iota(jnp.int32, shape, axis)


def pieces(value, count, axis):
    out = []
    for _ in range(count):
        part = value.astype(BF16)
        value = value - part.astype(F32)
        out.append(part)
    return jnp.concatenate(out, axis=axis)


def kernel(chips, ring, x_ref, ld_any, b_any, c_any, skip_any, dy_ref,
           y_ref, dx_ref, gld_ref, gb_ref, gc_ref,
           xv, dyv, b_ref, c_ref, ld_ref, skip_ref,
           xs, ds, a_exp, inv_exp, gmat, hmat, sp, tp, mm, mt, dcs, dbs, bnd,
           spread, parts_a, parts_i, rows, heads_of, tri_s, skipe,
           state, grad, th, tb, lamh, lamp, pf, pb, cmf, cmb, rf, rb, esf, esb,
           ref_, reb, p2f, p2b, pef, peb, rsbuf,
           in_s, lam_s, lam_r, pair_s, pair_r, a2a_s, a2a_r, rs_s, rs_r):
    seq = lax.axis_index("seq")
    z = lax.axis_index("exp")
    core = lax.rem(seq, 2)
    chip = seq // 2
    other = 1 - core
    partner = (chip * 2 + other, z)
    heads = ld_ref.shape[0]
    length, width = x_ref.shape
    nc = ring
    q = length // nc
    nx = min(4, chips)
    ny = chips // nx
    cx, cy = lax.rem(chip, nx), chip // nx
    state_n = b_ref.shape[1]
    pr = state_n // chips
    half = width // 2
    lb = half // LANES
    kh = nc * heads
    far = ring // 2

    def chip_dev(p):
        return (p * 2 + core, z)

    offsets = sorted(
        [(dy, dx) for dy in range(ny) for dx in range(nx) if (dy, dx) != (0, 0)],
        key=lambda o: (min(o[0], ny - o[0]) + min(o[1], nx - o[1]), o[0]))
    count = len(offsets)

    def chip_to(d):
        dy, dx = offsets[d]
        return lax.rem(cy + dy, ny) * nx + lax.rem(cx + dx, nx)

    def chip_from(d):
        dy, dx = offsets[d]
        return lax.rem(cy + ny - dy, ny) * nx + lax.rem(cx + nx - dx, nx)

    def remote(src, dst, s_sem, r_sem, dev):
        return pltpu.make_async_remote_copy(
            src_ref=src, dst_ref=dst, send_sem=s_sem, recv_sem=r_sem,
            device_id=dev, device_id_type=MESH)

    def rows_of(c):
        return pl.ds(pl.multiple_of(c * q, q), q)

    quart = length // 4

    def loads(k, part):
        src, dst = ((x_ref, xv), (dy_ref, dyv))[k]
        span = pl.ds(part * quart, quart)
        return pltpu.make_async_copy(src.at[span], dst.at[span], in_s.at[k, part])

    def whole_load(k):
        src, dst = ((b_any, b_ref), (c_any, c_ref), (ld_any, ld_ref), (skip_any, skip_ref))[k]
        return pltpu.make_async_copy(src, dst, in_s.at[k % 2, 4 + k // 2])

    whole_load(2).start()
    for part in range(4):
        loads(0, part).start()
    for k in (0, 1, 3):
        whole_load(k).start()
    for part in range(4):
        loads(1, part).start()

    barrier = pltpu.get_barrier_semaphore()
    pl.semaphore_signal(barrier, inc=1, device_id=partner, device_id_type=MESH)
    for d in range(count):
        pl.semaphore_signal(barrier, inc=1, device_id=chip_dev(chip_to(d)), device_id_type=MESH)
    z_dn = lax.rem(z + ring - 1, ring)
    z_up = lax.rem(z + 1, ring)
    pl.semaphore_signal(barrier, inc=1, device_id=(seq, z_dn), device_id_type=MESH)
    pl.semaphore_signal(barrier, inc=1, device_id=(seq, z_up), device_id_type=MESH)

    def head_of(shape, axis):
        return lax.shift_right_logical(iota(shape, axis), HEAD.bit_length() - 1)

    lane_heads = heads.bit_length() - 1
    one = ((iota((kh, width), 0) & (heads - 1)) == head_of((kh, width), 1)).astype(BF16)
    spread[0:kh, :] = one
    spread[kh:2 * kh, :] = one
    tri = (iota((q, q), 0) >= iota((q, q), 1)).astype(BF16)
    tri3 = jnp.concatenate([tri] * 3, axis=1)
    own_row = lax.shift_right_logical(iota((nc, kh), 1), lane_heads) == iota((nc, kh), 0)
    lane_chunk = lax.shift_right_logical(iota((q, 2 * kh), 1) & (kh - 1), lane_heads)

    whole_load(2).wait()
    stacked = jnp.concatenate([ld_ref[:, c * q:(c + 1) * q] for c in range(nc)], axis=0)
    cum = nt(tri3, pieces(stacked, 3, 1))
    rho = cum[q // 2 - 1:q // 2, :]
    tot = cum[q - 1:q, :]
    shifted = cum - rho
    parts_i[...] = pieces(jnp.exp(-shifted), 2, 1)
    parts_a[...] = pieces(jnp.exp(shifted), 2, 1)

    def by_chunk(parts):
        return jnp.concatenate(
            [jnp.where(lane_chunk == c, parts[...], jnp.zeros((), BF16)) for c in range(nc)], axis=0)

    inv_exp[...] = nn(by_chunk(parts_i), spread[...])
    pair_rows = jnp.concatenate(
        [jnp.where(own_row, jnp.exp(rho), 0.0), jnp.where(own_row, jnp.exp(tot - rho), 0.0)], axis=0)
    rows[...] = nn(pieces(pair_rows, 3, 1), jnp.concatenate([one, one, one], axis=0))
    both = rows[0:nc, :] * rows[nc:2 * nc, :]
    total = both[0:1, :]
    for c in range(1, nc):
        total = total * both[c:c + 1, :]
    for h in range(2):
        for r in range(lb):
            lamh[h, r:r + 1, :] = total[:, h * half + r * LANES:h * half + (r + 1) * LANES]

    def fwd_local(c):
        if c % (nc // 4) == 0:
            loads(0, c // (nc // 4)).wait()
        rc = slice(c * q, (c + 1) * q)
        scaled = (xv[rc, :].astype(F32) * inv_exp[rc, :]).astype(BF16)
        xs[c] = scaled
        got = tn(b_ref[rc, :], scaled)
        gmat[c] = got
        f = rows[c:c + 1, :]
        g = rows[nc + c:nc + c + 1, :]
        state[...] = g * got if c == 0 else g * (f * state[...] + got)

    def bwd_local(c):
        if (c + 1) % (nc // 4) == 0:
            loads(1, c // (nc // 4)).wait()
        rc = slice(c * q, (c + 1) * q)
        scaled = (dyv[rc, :].astype(F32) * a_exp[rc, :]).astype(BF16)
        ds[c] = scaled
        got = tn(c_ref[rc, :], scaled)
        hmat[c] = got
        f = rows[c:c + 1, :]
        g = rows[nc + c:nc + c + 1, :]
        grad[...] = f * got if c == nc - 1 else f * (g * grad[...] + got)

    def to_halves(src, dst):
        for h in range(2):
            for r in range(lb):
                lo = h * half + r * LANES
                dst[h, :, r * pr:(r + 1) * pr, :] = src[:, lo:lo + LANES].reshape(chips, pr, LANES)

    first = core == 0

    def piece_of(d):
        return chip_to(d) if d < count else chip

    def pair_send(base, src, dst, which):
        out = []
        for d in range(count + 1):
            p = which(d)
            out.append(remote(src.at[p], dst.at[p], pair_s.at[base, d], pair_r.at[base, d], partner))
            out[-1].start()
        return out

    def pass_on(base, d, src, dst, p):
        copy = remote(src.at[p], dst.at[chip], a2a_s.at[base, d], a2a_r.at[base, d], chip_dev(p))
        copy.start()
        return copy

    def lam_rows():
        return ([lamh[core, r:r + 1, :] for r in range(lb)], [lamp[r:r + 1, :] for r in range(lb)])

    def combine(base, came, kept, got, out, dst, forward):
        lo_, lp_ = lam_rows()
        go = []
        for d in range(count + 1):
            p = piece_of(d)
            came[d].wait_recv()
            for r in range(lb):
                lanes = slice(r * pr, (r + 1) * pr)
                mine, theirs = kept[core, p, lanes, :], got[p, lanes, :]
                if forward:
                    value = jnp.where(first, lp_[r], 1.0) * mine + jnp.where(first, 1.0, lo_[r]) * theirs
                else:
                    value = jnp.where(first, 1.0, lp_[r]) * mine + jnp.where(first, lo_[r], 1.0) * theirs
                if d < count:
                    out[p, lanes, :] = value
                else:
                    dst[chip, lanes, :] = value
            if forward:
                for r in range(lb):
                    row = slice(lb * pr + r, lb * pr + r + 1)
                    if d < count:
                        out[p, row, :] = lo_[r] * lp_[r]
                    else:
                        dst[chip, row, :] = lo_[r] * lp_[r]
            if d < count:
                go.append(pass_on(base, d, out, dst, p))
        return go

    def scan_pieces(go, base, got, out, dst, order):
        for copy in go:
            copy.wait_recv()
        run = [jnp.zeros((pr, LANES), F32) for _ in range(lb)]
        for p in order:
            for r in range(lb):
                out[p, r * pr:(r + 1) * pr, :] = run[r]
                run[r] = rf[p, lb * pr + r:lb * pr + r + 1, :] * run[r] + got[p, r * pr:(r + 1) * pr, :]
        dst[chip] = out[chip]
        return [pass_on(base, d, out, dst, chip_to(d)) for d in range(count)]

    def place(dst, p, r, lane_half, value):
        lo = pl.multiple_of(lane_half * half + r * LANES, LANES)
        dst[pl.ds(pl.multiple_of(p * pr, pr), pr), pl.ds(lo, LANES)] = value

    def hand_out(base, ret, enters, kept, got, share, shared, dst, forward):
        lo_, lp_ = lam_rows()
        out = []
        for d in [count, *range(count)]:
            p = chip_from(d) if d < count else chip
            if d < count:
                ret[d].wait_recv()
            for r in range(lb):
                lanes = slice(r * pr, (r + 1) * pr)
                enter = enters[p, lanes, :]
                if forward:
                    past = jnp.where(first, lo_[r], lp_[r]) * enter + jnp.where(
                        first, kept[core, p, lanes, :], got[p, lanes, :])
                    own, theirs = jnp.where(first, enter, past), jnp.where(first, past, enter)
                else:
                    past = jnp.where(first, lp_[r], lo_[r]) * enter + jnp.where(
                        first, got[p, lanes, :], kept[core, p, lanes, :])
                    own, theirs = jnp.where(first, past, enter), jnp.where(first, enter, past)
                share[p, lanes, :] = theirs
                place(dst, p, r, core, own)
            copy = remote(share.at[p], shared.at[p], pair_s.at[base, d], pair_r.at[base, d], partner)
            copy.start()
            out.append((p, copy))
        return out

    def take_in(pairs, shared, dst):
        for p, copy in pairs:
            copy.wait_recv()
            for r in range(lb):
                place(dst, p, r, other, shared[p, r * pr:(r + 1) * pr, :])

    lower = iota((q, q), 0) >= iota((q, q), 1)
    upper = iota((q, q), 0) <= iota((q, q), 1)

    def inner(c):
        rc = slice(c * q, (c + 1) * q)
        bb, cc = b_ref[rc, :], c_ref[rc, :]
        mm[c] = jnp.where(lower, nt(cc, bb), 0.0).astype(BF16)
        mt[c] = jnp.where(upper, nt(bb, cc), 0.0).astype(BF16)
        dm = jnp.where(lower, nt(ds[c], xs[c]), 0.0).astype(BF16)
        dcs[c] = nn(dm, bb)
        dbs[c] = tn(dm, cc)

    whole_load(0).wait()
    for c in range(nc):
        fwd_local(c)
    to_halves(state, th)
    pl.semaphore_wait(barrier, chips + 2)
    send_lam = remote(lamh.at[other], lamp, lam_s, lam_r, partner)
    send_lam.start()
    pair_f = pair_send(0, th.at[other], pf, piece_of)
    whole_load(1).wait()
    a_exp[...] = nn(by_chunk(parts_a), spread[...])
    for c in reversed(range(nc)):
        bwd_local(c)
    to_halves(grad, tb)
    pair_b = pair_send(1, tb.at[other], pb, piece_of)
    whole_load(3).wait()
    send_lam.wait_recv()
    go_f = combine(0, pair_f, th, pf, cmf, rf, True)
    go_b = combine(1, pair_b, tb, pb, cmb, rb, False)
    for c in range(nc // 2):
        inner(c)
    ret_f = scan_pieces(go_f, 2, rf, esf, ref_, range(chips))
    for c in range(nc // 2, 3 * nc // 4):
        inner(c)
    ret_b = scan_pieces(go_b, 3, rb, esb, reb, list(reversed(range(chips))))
    for c in range(3 * nc // 4, nc):
        inner(c)
    tri_s[...] = jnp.concatenate([tri] * 3, axis=0)
    head_one = (head_of((heads, width), 1) == iota((heads, width), 0)).astype(BF16)
    skipe[...] = nn(pieces(skip_ref[...], 3, 1), jnp.concatenate([head_one] * 3, axis=0))
    col = (head_of((width, heads), 0) == iota((width, heads), 1)).astype(BF16)
    heads_of[...] = jnp.concatenate([col, col], axis=0)
    send_2f = hand_out(2, ret_f, ref_, th, pf, p2f, pef, state, True)
    take_in(send_2f, pef, state)

    for c in range(nc):
        entering = rows[c:c + 1, :] * state[...]
        sp[c] = entering.astype(BF16)
        leaving = entering + gmat[c]
        gmat[c] = leaving
        state[...] = rows[nc + c:nc + c + 1, :] * leaving

    hq = q // 2
    started = {}

    def chunk_at(way, step):
        gap = far - step
        return lax.rem(z + (ring - gap if way == 0 else gap), ring)

    def rs_send(t, own, way, step, long):
        lo = (way if long else 1 - way) * hq
        first_step = 0 if long else 1
        k = chunk_at(way, step)
        if step == first_step:
            src = own.at[k, pl.ds(lo, hq)]
        else:
            started[t, way, step - 1, long].wait_recv()
            rsbuf[t, way, step - 1, lo:lo + hq, :] += own[k, lo:lo + hq, :]
            src = rsbuf.at[t, way, step - 1, pl.ds(lo, hq)]
        copy = remote(src, rsbuf.at[t, way, step, pl.ds(lo, hq)],
                      rs_s.at[t, way, step, int(long)], rs_r.at[t, way, step, int(long)],
                      (seq, z_dn if way == 0 else z_up))
        copy.start()
        started[t, way, step, long] = copy

    def rs_poll(t, own, step):
        for way in range(2):
            rs_send(t, own, way, step, True)
        if step + 1 < far:
            for way in range(2):
                rs_send(t, own, way, step + 1, False)

    def rs_end(t, own, out):
        for way in range(2):
            for long in (False, True):
                started[t, way, far - 1, long].wait_recv()
        out[...] = own[z] + rsbuf[t, 0, far - 1] + rsbuf[t, 1, far - 1]

    def near(i):
        gap = far - (i + 1) // 2
        return lax.rem(z + (gap if i % 2 == 1 else ring - gap), ring)

    def dc_chunk(i):
        c = near(i)
        dcs[c] += nt(ds[c], sp[c])

    def db_chunk(i):
        c = near(i)
        dbs[c] += nt(xs[c], tp[c])

    send_2b = hand_out(3, ret_b, reb, tb, pb, p2b, peb, grad, False)
    for i in range(3):
        dc_chunk(i)
    rs_poll(0, dcs, 0)
    for i in range(3, min(5, nc)):
        dc_chunk(i)
    take_in(send_2b, peb, grad)

    for c in reversed(range(nc)):
        later = rows[nc + c:nc + c + 1, :] * grad[...]
        low = later.astype(BF16)
        tp[c] = low
        bnd[c:c + 1, :] = jnp.sum(low.astype(F32) * gmat[c], axis=0, keepdims=True)
        if c:
            grad[...] = rows[c:c + 1, :] * (later + hmat[c])
    for i in range(3):
        db_chunk(i)
    rs_poll(1, dbs, 0)
    for i in range(5, nc):
        dc_chunk(i)
    for i in range(3, nc):
        db_chunk(i)
    rs_poll(0, dcs, 1)

    last_row = iota((q, width), 0) == q - 1

    def outputs(c):
        rc = slice(c * q, (c + 1) * q)
        x_c, d_c = xs[c], ds[c]
        acc_y = nn(jnp.concatenate([mm[c], c_ref[rc, :]], axis=1),
                   jnp.concatenate([x_c, sp[c]], axis=0))
        acc_x = nn(jnp.concatenate([mt[c], b_ref[rc, :]], axis=1),
                   jnp.concatenate([d_c, tp[c]], axis=0))
        gain = skipe[...]
        y_ref[rc, :] = (a_exp[rc, :] * acc_y + gain * xv[rc, :].astype(F32)).astype(BF16)
        dx_ref[rc, :] = (inv_exp[rc, :] * acc_x + gain * dyv[rc, :].astype(F32)).astype(BF16)
        diff = d_c.astype(F32) * acc_y - x_c.astype(F32) * acc_x
        diff = diff + jnp.where(last_row, bnd[c:c + 1, :], 0.0)
        per_head = nn(pieces(diff, 2, 1), heads_of[...])
        gld_ref[:, rc] = tn(pieces(per_head, 3, 0), tri_s[...])

    done = 0
    for step in range(1, far):
        upto = nc * step // far
        for c in range(done, upto):
            outputs(c)
        done = upto
        rs_poll(1, dbs, step)
        if step + 1 < far:
            rs_poll(0, dcs, step + 1)
    for c in range(done, nc):
        outputs(c)
    rs_end(0, dcs, gc_ref)
    rs_end(1, dbs, gb_ref)
    for copy in [send_lam, *pair_f, *pair_b, *go_f, *go_b, *ret_f, *ret_b,
                 *[c for _, c in send_2f], *[c for _, c in send_2b], *started.values()]:
        copy.wait_send()


def finish_kernel(*refs):
    count = (len(refs) - 1) // 2
    sems = refs[-1]
    copies = []
    for k in range(count):
        src, dst = refs[k], refs[count + k]
        parts = 4 if src.shape[0] >= 1024 else 1
        size = src.shape[0] // parts
        for i in range(parts):
            rows = pl.ds(i * size, size)
            copies.append(pltpu.make_async_copy(src.at[rows], dst.at[rows], sems.at[k, i]))
    for copy in copies:
        copy.start()
    for copy in copies:
        copy.wait()


def finish(arrays):
    return pl.pallas_call(
        finish_kernel,
        out_shape=tuple(jax.ShapeDtypeStruct(a.shape, a.dtype) for a in arrays),
        in_specs=[pl.BlockSpec(memory_space=pltpu.VMEM)] * len(arrays),
        out_specs=(pl.BlockSpec(memory_space=pl.ANY),) * len(arrays),
        scratch_shapes=[pltpu.SemaphoreType.DMA((len(arrays), 4))],
        compiler_params=pltpu.CompilerParams(vmem_limit_bytes=16 * 1024 * 1024),
    )(*arrays)


def body(chips, ring, mixer_input, log_decay, b_rows, c_rows, skip_gain, grad_out):
    length, width = mixer_input.shape
    heads = log_decay.shape[0]
    state_n = b_rows.shape[1]
    nc = ring
    q = length // nc
    kh = nc * heads
    pr = state_n // chips
    lb = width // 2 // LANES
    far = ring // 2
    vm = pltpu.VMEM
    msg = (chips, lb * pr, LANES)
    msg_l = (chips, lb * pr + 8, LANES)
    scratch = [
        vm((length, width), BF16), vm((length, width), BF16),
        vm((length, state_n), BF16), vm((length, state_n), BF16),
        vm((heads, length), F32), vm((1, heads), F32),
        vm((nc, q, width), BF16), vm((nc, q, width), BF16),
        vm((length, width), F32), vm((length, width), F32),
        vm((nc, state_n, width), F32), vm((nc, state_n, width), F32),
        vm((nc, state_n, width), BF16), vm((nc, state_n, width), BF16),
        vm((nc, q, q), BF16), vm((nc, q, q), BF16),
        vm((nc, q, state_n), F32), vm((nc, q, state_n), F32),
        vm((nc, width), F32),
        vm((2 * kh, width), BF16), vm((q, 2 * kh), BF16), vm((q, 2 * kh), BF16),
        vm((2 * nc, width), F32), vm((2 * width, heads), BF16), vm((3 * q, q), BF16), vm((1, width), F32),
        vm((state_n, width), F32), vm((state_n, width), F32),
        vm((2, *msg), F32), vm((2, *msg), F32), vm((2, 8, LANES), F32), vm((8, LANES), F32),
        vm(msg, F32), vm(msg, F32),
        vm(msg_l, F32), vm(msg, F32), vm(msg_l, F32), vm(msg, F32), vm(msg, F32), vm(msg, F32),
        vm(msg, F32), vm(msg, F32), vm(msg, F32), vm(msg, F32), vm(msg, F32), vm(msg, F32),
        vm((2, 2, far, q, state_n), F32),
        pltpu.SemaphoreType.DMA((2, 6)),
        pltpu.SemaphoreType.DMA, pltpu.SemaphoreType.DMA,
        pltpu.SemaphoreType.DMA((4, chips)), pltpu.SemaphoreType.DMA((4, chips)),
        pltpu.SemaphoreType.DMA((4, chips)), pltpu.SemaphoreType.DMA((4, chips)),
        pltpu.SemaphoreType.DMA((2, 2, far, 2)), pltpu.SemaphoreType.DMA((2, 2, far, 2)),
    ]
    whole = pl.BlockSpec(memory_space=pltpu.VMEM)
    outside = pl.BlockSpec(memory_space=pltpu.HBM)
    return finish(pl.pallas_call(
        functools.partial(kernel, chips, ring),
        out_shape=(
            vm((length, width), BF16),
            vm((length, width), BF16),
            vm((heads, length), F32),
            vm((q, state_n), F32),
            vm((q, state_n), F32),
        ),
        in_specs=[outside] * 6,
        out_specs=(whole,) * 5,
        scratch_shapes=scratch,
        compiler_params=pltpu.CompilerParams(
            collective_id=0, has_side_effects=True, vmem_limit_bytes=48 * 1024 * 1024),
    )(*[pltpu.with_memory_space_constraint(a, pltpu.HBM) for a in (
        mixer_input, log_decay, b_rows, c_rows, skip_gain.reshape(1, heads), grad_out)]))


def solution(mesh):
    chips = mesh.shape["seq"] // 2
    ring = mesh.shape["exp"]
    return jax.shard_map(
        functools.partial(body, chips, ring),
        mesh=mesh,
        in_specs=(
            P("seq", "exp"),
            P("exp", "seq"),
            P("seq", None),
            P("seq", None),
            P("exp"),
            P("seq", "exp"),
        ),
        out_specs=(
            P("seq", "exp"),
            P("seq", "exp"),
            P("exp", "seq"),
            P(("seq", "exp"), None),
            P(("seq", "exp"), None),
        ),
        check_vma=False,
    )
```

```python
import functools

import jax
import jax.numpy as jnp
from jax import lax
from jax.experimental import pallas as pl
from jax.experimental.pallas import tpu as pltpu
from jax.sharding import PartitionSpec as P

F32 = jnp.float32
BF16 = jnp.bfloat16
MESH = pl.DeviceIdType.MESH
HEAD = 64
LANES = 128


def dot(a, b, ca, cb):
    return lax.dot_general(a, b, (((ca,), (cb,)), ((), ())), preferred_element_type=F32)


def nn(a, b):
    return dot(a, b, 1, 0)


def nt(a, b):
    return dot(a, b, 1, 1)


def tn(a, b):
    return dot(a, b, 0, 0)


def iota(shape, axis):
    return lax.broadcasted_iota(jnp.int32, shape, axis)


def pieces(value, count, axis):
    out = []
    for _ in range(count):
        part = value.astype(BF16)
        value = value - part.astype(F32)
        out.append(part)
    return jnp.concatenate(out, axis=axis)


def kernel(chips, ring, x_ref, ld_any, b_any, c_any, skip_any, dy_ref,
           y_ref, dx_ref, gld_ref, gb_ref, gc_ref,
           xv, dyv, b_ref, c_ref, ld_ref, skip_ref,
           xs, ds, a_exp, inv_exp, gmat, hmat, sp, tp, mm, mt, dcs, dbs, bnd,
           spread, parts_a, parts_i, rows, heads_of, tri_s, skipe,
           state, grad, th, tb, lamh, lamp, pf, pb, cmf, cmb, rf, rb, esf, esb,
           ref_, reb, p2f, p2b, pef, peb, rsbuf, rsout,
           in_s, lam_s, lam_r, pair_s, pair_r, a2a_s, a2a_r, rs_s, rs_r):
    seq = lax.axis_index("seq")
    z = lax.axis_index("exp")
    core = lax.rem(seq, 2)
    chip = seq // 2
    other = 1 - core
    partner = (chip * 2 + other, z)
    heads = ld_ref.shape[0]
    length, width = x_ref.shape
    nc = ring
    q = length // nc
    nx = min(4, chips)
    ny = chips // nx
    cx, cy = lax.rem(chip, nx), chip // nx
    state_n = b_ref.shape[1]
    pr = state_n // chips
    half = width // 2
    lb = half // LANES
    kh = nc * heads
    far = ring // 2

    def chip_dev(p):
        return (p * 2 + core, z)

    offsets = sorted(
        [(dy, dx) for dy in range(ny) for dx in range(nx) if (dy, dx) != (0, 0)],
        key=lambda o: (min(o[0], ny - o[0]) + min(o[1], nx - o[1]), o[0]))
    count = len(offsets)

    def chip_to(d):
        dy, dx = offsets[d]
        return lax.rem(cy + dy, ny) * nx + lax.rem(cx + dx, nx)

    def chip_from(d):
        dy, dx = offsets[d]
        return lax.rem(cy + ny - dy, ny) * nx + lax.rem(cx + nx - dx, nx)

    def remote(src, dst, s_sem, r_sem, dev):
        return pltpu.make_async_remote_copy(
            src_ref=src, dst_ref=dst, send_sem=s_sem, recv_sem=r_sem,
            device_id=dev, device_id_type=MESH)

    def rows_of(c):
        return pl.ds(pl.multiple_of(c * q, q), q)

    quart = length // 4

    def loads(k, part):
        src, dst = ((x_ref, xv), (dy_ref, dyv))[k]
        span = pl.ds(part * quart, quart)
        return pltpu.make_async_copy(src.at[span], dst.at[span], in_s.at[k, part])

    def whole_load(k):
        src, dst = ((b_any, b_ref), (c_any, c_ref), (ld_any, ld_ref), (skip_any, skip_ref))[k]
        return pltpu.make_async_copy(src, dst, in_s.at[k % 2, 4 + k // 2])

    whole_load(2).start()
    for part in range(4):
        loads(0, part).start()
    for k in (0, 1, 3):
        whole_load(k).start()
    for part in range(4):
        loads(1, part).start()

    barrier = pltpu.get_barrier_semaphore()
    pl.semaphore_signal(barrier, inc=1, device_id=partner, device_id_type=MESH)
    for d in range(count):
        pl.semaphore_signal(barrier, inc=1, device_id=chip_dev(chip_to(d)), device_id_type=MESH)
    relay = far // 2
    for hop in range(1, relay + 1):
        for to in (lax.rem(z + hop, ring), lax.rem(z + ring - hop, ring)):
            pl.semaphore_signal(barrier, inc=1, device_id=(seq, to), device_id_type=MESH)

    def head_of(shape, axis):
        return lax.shift_right_logical(iota(shape, axis), HEAD.bit_length() - 1)

    lane_heads = heads.bit_length() - 1
    one = ((iota((kh, width), 0) & (heads - 1)) == head_of((kh, width), 1)).astype(BF16)
    spread[0:kh, :] = one
    spread[kh:2 * kh, :] = one
    tri = (iota((q, q), 0) >= iota((q, q), 1)).astype(BF16)
    tri3 = jnp.concatenate([tri] * 3, axis=1)
    own_row = lax.shift_right_logical(iota((nc, kh), 1), lane_heads) == iota((nc, kh), 0)
    lane_chunk = lax.shift_right_logical(iota((q, 2 * kh), 1) & (kh - 1), lane_heads)

    whole_load(2).wait()
    stacked = jnp.concatenate([ld_ref[:, c * q:(c + 1) * q] for c in range(nc)], axis=0)
    cum = nt(tri3, pieces(stacked, 3, 1))
    rho = cum[q // 2 - 1:q // 2, :]
    tot = cum[q - 1:q, :]
    shifted = cum - rho
    parts_i[...] = pieces(jnp.exp(-shifted), 2, 1)
    parts_a[...] = pieces(jnp.exp(shifted), 2, 1)

    def by_chunk(parts):
        return jnp.concatenate(
            [jnp.where(lane_chunk == c, parts[...], jnp.zeros((), BF16)) for c in range(nc)], axis=0)

    inv_exp[...] = nn(by_chunk(parts_i), spread[...])
    pair_rows = jnp.concatenate(
        [jnp.where(own_row, jnp.exp(rho), 0.0), jnp.where(own_row, jnp.exp(tot - rho), 0.0)], axis=0)
    rows[...] = nn(pieces(pair_rows, 3, 1), jnp.concatenate([one, one, one], axis=0))
    both = rows[0:nc, :] * rows[nc:2 * nc, :]
    total = both[0:1, :]
    for c in range(1, nc):
        total = total * both[c:c + 1, :]
    for h in range(2):
        for r in range(lb):
            lamh[h, r:r + 1, :] = total[:, h * half + r * LANES:h * half + (r + 1) * LANES]

    def fwd_local(c):
        if c % (nc // 4) == 0:
            loads(0, c // (nc // 4)).wait()
        rc = slice(c * q, (c + 1) * q)
        scaled = (xv[rc, :].astype(F32) * inv_exp[rc, :]).astype(BF16)
        xs[c] = scaled
        got = tn(b_ref[rc, :], scaled)
        gmat[c] = got
        f = rows[c:c + 1, :]
        g = rows[nc + c:nc + c + 1, :]
        state[...] = g * got if c == 0 else g * (f * state[...] + got)

    def bwd_local(c):
        if (c + 1) % (nc // 4) == 0:
            loads(1, c // (nc // 4)).wait()
        rc = slice(c * q, (c + 1) * q)
        scaled = (dyv[rc, :].astype(F32) * a_exp[rc, :]).astype(BF16)
        ds[c] = scaled
        got = tn(c_ref[rc, :], scaled)
        hmat[c] = got
        f = rows[c:c + 1, :]
        g = rows[nc + c:nc + c + 1, :]
        grad[...] = f * got if c == nc - 1 else f * (g * grad[...] + got)

    def to_halves(src, dst):
        for h in range(2):
            for r in range(lb):
                lo = h * half + r * LANES
                dst[h, :, r * pr:(r + 1) * pr, :] = src[:, lo:lo + LANES].reshape(chips, pr, LANES)

    first = core == 0

    def piece_of(d):
        return chip_to(d) if d < count else chip

    def pair_send(base, src, dst, which):
        out = []
        for d in range(count + 1):
            p = which(d)
            out.append(remote(src.at[p], dst.at[p], pair_s.at[base, d], pair_r.at[base, d], partner))
            out[-1].start()
        return out

    def pass_on(base, d, src, dst, p):
        copy = remote(src.at[p], dst.at[chip], a2a_s.at[base, d], a2a_r.at[base, d], chip_dev(p))
        copy.start()
        return copy

    def lam_rows():
        return ([lamh[core, r:r + 1, :] for r in range(lb)], [lamp[r:r + 1, :] for r in range(lb)])

    def combine(base, came, kept, got, out, dst, forward):
        lo_, lp_ = lam_rows()
        go = []
        for d in range(count + 1):
            p = piece_of(d)
            came[d].wait_recv()
            for r in range(lb):
                lanes = slice(r * pr, (r + 1) * pr)
                mine, theirs = kept[core, p, lanes, :], got[p, lanes, :]
                if forward:
                    value = jnp.where(first, lp_[r], 1.0) * mine + jnp.where(first, 1.0, lo_[r]) * theirs
                else:
                    value = jnp.where(first, 1.0, lp_[r]) * mine + jnp.where(first, lo_[r], 1.0) * theirs
                if d < count:
                    out[p, lanes, :] = value
                else:
                    dst[chip, lanes, :] = value
            if forward:
                for r in range(lb):
                    row = slice(lb * pr + r, lb * pr + r + 1)
                    if d < count:
                        out[p, row, :] = lo_[r] * lp_[r]
                    else:
                        dst[chip, row, :] = lo_[r] * lp_[r]
            if d < count:
                go.append(pass_on(base, d, out, dst, p))
        return go

    def scan_pieces(go, base, got, out, dst, order):
        for copy in go:
            copy.wait_recv()
        run = [jnp.zeros((pr, LANES), F32) for _ in range(lb)]
        for p in order:
            for r in range(lb):
                out[p, r * pr:(r + 1) * pr, :] = run[r]
                run[r] = rf[p, lb * pr + r:lb * pr + r + 1, :] * run[r] + got[p, r * pr:(r + 1) * pr, :]
        dst[chip] = out[chip]
        return [pass_on(base, d, out, dst, chip_to(d)) for d in range(count)]

    def place(dst, p, r, lane_half, value):
        lo = pl.multiple_of(lane_half * half + r * LANES, LANES)
        dst[pl.ds(pl.multiple_of(p * pr, pr), pr), pl.ds(lo, LANES)] = value

    def hand_out(base, ret, enters, kept, got, share, shared, dst, forward):
        lo_, lp_ = lam_rows()
        out = []
        for d in [count, *range(count)]:
            p = chip_from(d) if d < count else chip
            if d < count:
                ret[d].wait_recv()
            for r in range(lb):
                lanes = slice(r * pr, (r + 1) * pr)
                enter = enters[p, lanes, :]
                if forward:
                    past = jnp.where(first, lo_[r], lp_[r]) * enter + jnp.where(
                        first, kept[core, p, lanes, :], got[p, lanes, :])
                    own, theirs = jnp.where(first, enter, past), jnp.where(first, past, enter)
                else:
                    past = jnp.where(first, lp_[r], lo_[r]) * enter + jnp.where(
                        first, got[p, lanes, :], kept[core, p, lanes, :])
                    own, theirs = jnp.where(first, past, enter), jnp.where(first, enter, past)
                share[p, lanes, :] = theirs
                place(dst, p, r, core, own)
            copy = remote(share.at[p], shared.at[p], pair_s.at[base, d], pair_r.at[base, d], partner)
            copy.start()
            out.append((p, copy))
        return out

    def take_in(pairs, shared, dst):
        for p, copy in pairs:
            copy.wait_recv()
            for r in range(lb):
                place(dst, p, r, other, shared[p, r * pr:(r + 1) * pr, :])

    lower = iota((q, q), 0) >= iota((q, q), 1)
    upper = iota((q, q), 0) <= iota((q, q), 1)

    def inner(c):
        rc = slice(c * q, (c + 1) * q)
        bb, cc = b_ref[rc, :], c_ref[rc, :]
        mm[c] = jnp.where(lower, nt(cc, bb), 0.0).astype(BF16)
        mt[c] = jnp.where(upper, nt(bb, cc), 0.0).astype(BF16)
        dm = jnp.where(lower, nt(ds[c], xs[c]), 0.0).astype(BF16)
        dcs[c] = nn(dm, bb)
        dbs[c] = tn(dm, cc)

    whole_load(0).wait()
    for c in range(nc):
        fwd_local(c)
    to_halves(state, th)
    pl.semaphore_wait(barrier, chips + 2 * relay)
    send_lam = remote(lamh.at[other], lamp, lam_s, lam_r, partner)
    send_lam.start()
    pair_f = pair_send(0, th.at[other], pf, piece_of)
    whole_load(1).wait()
    a_exp[...] = nn(by_chunk(parts_a), spread[...])
    for c in reversed(range(nc)):
        bwd_local(c)
    to_halves(grad, tb)
    pair_b = pair_send(1, tb.at[other], pb, piece_of)
    whole_load(3).wait()
    send_lam.wait_recv()
    go_f = combine(0, pair_f, th, pf, cmf, rf, True)
    go_b = combine(1, pair_b, tb, pb, cmb, rb, False)
    for c in range(nc // 2):
        inner(c)
    ret_f = scan_pieces(go_f, 2, rf, esf, ref_, range(chips))
    for c in range(nc // 2, 3 * nc // 4):
        inner(c)
    ret_b = scan_pieces(go_b, 3, rb, esb, reb, list(reversed(range(chips))))
    for c in range(3 * nc // 4, nc):
        inner(c)
    tri_s[...] = jnp.concatenate([tri] * 3, axis=0)
    head_one = (head_of((heads, width), 1) == iota((heads, width), 0)).astype(BF16)
    skipe[...] = nn(pieces(skip_ref[...], 3, 1), jnp.concatenate([head_one] * 3, axis=0))
    col = (head_of((width, heads), 0) == iota((width, heads), 1)).astype(BF16)
    heads_of[...] = jnp.concatenate([col, col], axis=0)
    send_2f = hand_out(2, ret_f, ref_, th, pf, p2f, pef, state, True)
    take_in(send_2f, pef, state)

    for c in range(nc):
        entering = rows[c:c + 1, :] * state[...]
        sp[c] = entering.astype(BF16)
        leaving = entering + gmat[c]
        gmat[c] = leaving
        state[...] = rows[nc + c:nc + c + 1, :] * leaving

    hq = q // 2
    started = {}

    def away(way, gap):
        return lax.rem(z + (ring - gap if way == 0 else gap), ring)

    def rows_at(way, gap):
        return pl.ds(way * hq, hq) if gap == far else pl.ds(0, q)

    def rs_send(t, way, gap, src):
        hop = gap - relay if gap > relay else gap
        span = rows_at(way, gap)
        copy = remote(src.at[span], rsbuf.at[t, way, gap - 1, span],
                      rs_s.at[t, way, gap - 1], rs_r.at[t, way, gap - 1], (seq, away(way, hop)))
        copy.start()
        started[t, way, gap] = copy

    def rs_first(t, own, gaps):
        for gap in gaps:
            for way in range(2):
                rs_send(t, way, gap, own.at[away(way, gap)])

    def rs_second(t, own):
        for way in range(2):
            for gap in range(relay + 1, far + 1):
                started[t, way, gap].wait_recv()
            k = away(way, relay)
            for side in range(2):
                span = slice(side * hq, (side + 1) * hq)
                value = own[k, span, :]
                for gap in range(relay + 1, far + 1):
                    if gap < far or side == way:
                        value = value + rsbuf[t, way, gap - 1, span, :]
                rsout[t, way, span, :] = value
            rs_send(t, way, relay, rsout.at[t, way])

    def rs_end(t, own, out):
        value = own[z]
        for gap in range(1, relay + 1):
            for way in range(2):
                started[t, way, gap].wait_recv()
                value = value + rsbuf[t, way, gap - 1]
        out[...] = value

    far_gaps = list(range(far, relay, -1))
    near_gaps = list(range(1, relay))
    order = [(0, far)] + [(way, g) for g in far_gaps[1:] + near_gaps + [relay] for way in range(2)]
    n_far = 1 + 2 * (len(far_gaps) - 1)
    n_first = n_far + 2 * len(near_gaps)

    def near(i):
        return away(*order[i]) if i < len(order) else z

    def dc_chunk(i):
        c = near(i)
        dcs[c] += nt(ds[c], sp[c])

    def db_chunk(i):
        c = near(i)
        dbs[c] += nt(xs[c], tp[c])

    send_2b = hand_out(3, ret_b, reb, tb, pb, p2b, peb, grad, False)
    for i in range(n_far):
        dc_chunk(i)
    rs_first(0, dcs, far_gaps)
    for i in range(n_far, n_first):
        dc_chunk(i)
    rs_first(0, dcs, near_gaps)
    take_in(send_2b, peb, grad)

    for c in reversed(range(nc)):
        later = rows[nc + c:nc + c + 1, :] * grad[...]
        low = later.astype(BF16)
        tp[c] = low
        bnd[c:c + 1, :] = jnp.sum(low.astype(F32) * gmat[c], axis=0, keepdims=True)
        if c:
            grad[...] = rows[c:c + 1, :] * (later + hmat[c])
    for i in range(n_far):
        db_chunk(i)
    rs_first(1, dbs, far_gaps)
    for i in range(n_far, n_first):
        db_chunk(i)
    rs_first(1, dbs, near_gaps)
    for i in range(n_first, nc):
        dc_chunk(i)
    for i in range(n_first, nc):
        db_chunk(i)

    last_row = iota((q, width), 0) == q - 1

    def outputs(c):
        rc = slice(c * q, (c + 1) * q)
        x_c, d_c = xs[c], ds[c]
        acc_y = nn(jnp.concatenate([mm[c], c_ref[rc, :]], axis=1),
                   jnp.concatenate([x_c, sp[c]], axis=0))
        acc_x = nn(jnp.concatenate([mt[c], b_ref[rc, :]], axis=1),
                   jnp.concatenate([d_c, tp[c]], axis=0))
        gain = skipe[...]
        y_ref[rc, :] = (a_exp[rc, :] * acc_y + gain * xv[rc, :].astype(F32)).astype(BF16)
        dx_ref[rc, :] = (inv_exp[rc, :] * acc_x + gain * dyv[rc, :].astype(F32)).astype(BF16)
        diff = d_c.astype(F32) * acc_y - x_c.astype(F32) * acc_x
        diff = diff + jnp.where(last_row, bnd[c:c + 1, :], 0.0)
        per_head = nn(pieces(diff, 2, 1), heads_of[...])
        gld_ref[:, rc] = tn(pieces(per_head, 3, 0), tri_s[...])

    for c in range(nc):
        outputs(c)
        if c == nc // 4 - 1:
            rs_second(0, dcs)
        if c == 3 * nc // 4 - 1:
            rs_second(1, dbs)
    rs_end(0, dcs, gc_ref)
    rs_end(1, dbs, gb_ref)
    for copy in [send_lam, *pair_f, *pair_b, *go_f, *go_b, *ret_f, *ret_b,
                 *[c for _, c in send_2f], *[c for _, c in send_2b], *started.values()]:
        copy.wait_send()


def finish_kernel(*refs):
    count = (len(refs) - 1) // 2
    sems = refs[-1]
    copies = []
    for k in range(count):
        src, dst = refs[k], refs[count + k]
        parts = 4 if src.shape[0] >= 1024 else 1
        size = src.shape[0] // parts
        for i in range(parts):
            rows = pl.ds(i * size, size)
            copies.append(pltpu.make_async_copy(src.at[rows], dst.at[rows], sems.at[k, i]))
    for copy in copies:
        copy.start()
    for copy in copies:
        copy.wait()


def finish(arrays):
    return pl.pallas_call(
        finish_kernel,
        out_shape=tuple(jax.ShapeDtypeStruct(a.shape, a.dtype) for a in arrays),
        in_specs=[pl.BlockSpec(memory_space=pltpu.VMEM)] * len(arrays),
        out_specs=(pl.BlockSpec(memory_space=pl.ANY),) * len(arrays),
        scratch_shapes=[pltpu.SemaphoreType.DMA((len(arrays), 4))],
        compiler_params=pltpu.CompilerParams(vmem_limit_bytes=16 * 1024 * 1024),
    )(*arrays)


def body(chips, ring, mixer_input, log_decay, b_rows, c_rows, skip_gain, grad_out):
    length, width = mixer_input.shape
    heads = log_decay.shape[0]
    state_n = b_rows.shape[1]
    nc = ring
    q = length // nc
    kh = nc * heads
    pr = state_n // chips
    lb = width // 2 // LANES
    far = ring // 2
    vm = pltpu.VMEM
    msg = (chips, lb * pr, LANES)
    msg_l = (chips, lb * pr + 8, LANES)
    scratch = [
        vm((length, width), BF16), vm((length, width), BF16),
        vm((length, state_n), BF16), vm((length, state_n), BF16),
        vm((heads, length), F32), vm((1, heads), F32),
        vm((nc, q, width), BF16), vm((nc, q, width), BF16),
        vm((length, width), F32), vm((length, width), F32),
        vm((nc, state_n, width), F32), vm((nc, state_n, width), F32),
        vm((nc, state_n, width), BF16), vm((nc, state_n, width), BF16),
        vm((nc, q, q), BF16), vm((nc, q, q), BF16),
        vm((nc, q, state_n), F32), vm((nc, q, state_n), F32),
        vm((nc, width), F32),
        vm((2 * kh, width), BF16), vm((q, 2 * kh), BF16), vm((q, 2 * kh), BF16),
        vm((2 * nc, width), F32), vm((2 * width, heads), BF16), vm((3 * q, q), BF16), vm((1, width), F32),
        vm((state_n, width), F32), vm((state_n, width), F32),
        vm((2, *msg), F32), vm((2, *msg), F32), vm((2, 8, LANES), F32), vm((8, LANES), F32),
        vm(msg, F32), vm(msg, F32),
        vm(msg_l, F32), vm(msg, F32), vm(msg_l, F32), vm(msg, F32), vm(msg, F32), vm(msg, F32),
        vm(msg, F32), vm(msg, F32), vm(msg, F32), vm(msg, F32), vm(msg, F32), vm(msg, F32),
        vm((2, 2, far, q, state_n), F32), vm((2, 2, q, state_n), F32),
        pltpu.SemaphoreType.DMA((2, 6)),
        pltpu.SemaphoreType.DMA, pltpu.SemaphoreType.DMA,
        pltpu.SemaphoreType.DMA((4, chips)), pltpu.SemaphoreType.DMA((4, chips)),
        pltpu.SemaphoreType.DMA((4, chips)), pltpu.SemaphoreType.DMA((4, chips)),
        pltpu.SemaphoreType.DMA((2, 2, far)), pltpu.SemaphoreType.DMA((2, 2, far)),
    ]
    whole = pl.BlockSpec(memory_space=pltpu.VMEM)
    outside = pl.BlockSpec(memory_space=pltpu.HBM)
    return finish(pl.pallas_call(
        functools.partial(kernel, chips, ring),
        out_shape=(
            vm((length, width), BF16),
            vm((length, width), BF16),
            vm((heads, length), F32),
            vm((q, state_n), F32),
            vm((q, state_n), F32),
        ),
        in_specs=[outside] * 6,
        out_specs=(whole,) * 5,
        scratch_shapes=scratch,
        compiler_params=pltpu.CompilerParams(
            collective_id=0, has_side_effects=True, vmem_limit_bytes=48 * 1024 * 1024),
    )(*[pltpu.with_memory_space_constraint(a, pltpu.HBM) for a in (
        mixer_input, log_decay, b_rows, c_rows, skip_gain.reshape(1, heads), grad_out)]))


def solution(mesh):
    chips = mesh.shape["seq"] // 2
    ring = mesh.shape["exp"]
    return jax.shard_map(
        functools.partial(body, chips, ring),
        mesh=mesh,
        in_specs=(
            P("seq", "exp"),
            P("exp", "seq"),
            P("seq", None),
            P("seq", None),
            P("exp"),
            P("seq", "exp"),
        ),
        out_specs=(
            P("seq", "exp"),
            P("seq", "exp"),
            P("exp", "seq"),
            P(("seq", "exp"), None),
            P(("seq", "exp"), None),
        ),
        check_vma=False,
    )
```

```python
import functools

import jax
import jax.numpy as jnp
from jax import lax
from jax.experimental import pallas as pl
from jax.experimental.pallas import tpu as pltpu
from jax.sharding import PartitionSpec as P

F32 = jnp.float32
BF16 = jnp.bfloat16
MESH = pl.DeviceIdType.MESH
HEAD = 64
LANES = 128


def dot(a, b, ca, cb):
    return lax.dot_general(a, b, (((ca,), (cb,)), ((), ())), preferred_element_type=F32)


def nn(a, b):
    return dot(a, b, 1, 0)


def nt(a, b):
    return dot(a, b, 1, 1)


def tn(a, b):
    return dot(a, b, 0, 0)


def iota(shape, axis):
    return lax.broadcasted_iota(jnp.int32, shape, axis)


def pieces(value, count, axis):
    out = []
    for _ in range(count):
        part = value.astype(BF16)
        value = value - part.astype(F32)
        out.append(part)
    return jnp.concatenate(out, axis=axis)


def kernel(chips, ring, x_ref, ld_any, b_any, c_any, skip_any, dy_ref,
           y_ref, dx_ref, gld_ref, gb_ref, gc_ref,
           xv, dyv, b_ref, c_ref, ld_ref, skip_ref,
           xs, ds, a_exp, inv_exp, gmat, hmat, sp, tp, mm, mt, dcs, dbs, bnd,
           spread, parts_a, parts_i, rows, heads_of, tri_s, skipe,
           state, grad, th, tb, lamh, lamp, pf, pb, cmf, cmb, rf, rb, esf, esb,
           ref_, reb, p2f, p2b, pef, peb, rsbuf,
           in_s, lam_s, lam_r, pair_s, pair_r, a2a_s, a2a_r, rs_s, rs_r):
    seq = lax.axis_index("seq")
    z = lax.axis_index("exp")
    core = lax.rem(seq, 2)
    chip = seq // 2
    other = 1 - core
    partner = (chip * 2 + other, z)
    heads = ld_ref.shape[0]
    length, width = x_ref.shape
    nc = ring
    q = length // nc
    nx = min(4, chips)
    ny = chips // nx
    cx, cy = lax.rem(chip, nx), chip // nx
    state_n = b_ref.shape[1]
    pr = state_n // chips
    half = width // 2
    lb = half // LANES
    kh = nc * heads
    far = ring // 2

    def chip_dev(p):
        return (p * 2 + core, z)

    offsets = sorted(
        [(dy, dx) for dy in range(ny) for dx in range(nx) if (dy, dx) != (0, 0)],
        key=lambda o: (min(o[0], ny - o[0]) + min(o[1], nx - o[1]), o[0]))
    count = len(offsets)

    def chip_to(d):
        dy, dx = offsets[d]
        return lax.rem(cy + dy, ny) * nx + lax.rem(cx + dx, nx)

    def chip_from(d):
        dy, dx = offsets[d]
        return lax.rem(cy + ny - dy, ny) * nx + lax.rem(cx + nx - dx, nx)

    def remote(src, dst, s_sem, r_sem, dev):
        return pltpu.make_async_remote_copy(
            src_ref=src, dst_ref=dst, send_sem=s_sem, recv_sem=r_sem,
            device_id=dev, device_id_type=MESH)

    def rows_of(c):
        return pl.ds(pl.multiple_of(c * q, q), q)

    quart = length // 4

    def loads(k, part):
        src, dst = ((x_ref, xv), (dy_ref, dyv))[k]
        span = pl.ds(part * quart, quart)
        return pltpu.make_async_copy(src.at[span], dst.at[span], in_s.at[k, part])

    def whole_load(k):
        src, dst = ((b_any, b_ref), (c_any, c_ref), (ld_any, ld_ref), (skip_any, skip_ref))[k]
        return pltpu.make_async_copy(src, dst, in_s.at[k % 2, 4 + k // 2])

    whole_load(2).start()
    for part in range(4):
        loads(0, part).start()
    for k in (0, 1, 3):
        whole_load(k).start()
    for part in range(4):
        loads(1, part).start()

    barrier = pltpu.get_barrier_semaphore()
    pl.semaphore_signal(barrier, inc=1, device_id=partner, device_id_type=MESH)
    for d in range(count):
        pl.semaphore_signal(barrier, inc=1, device_id=chip_dev(chip_to(d)), device_id_type=MESH)
    z_dn = lax.rem(z + ring - 1, ring)
    z_up = lax.rem(z + 1, ring)
    pl.semaphore_signal(barrier, inc=1, device_id=(seq, z_dn), device_id_type=MESH)
    pl.semaphore_signal(barrier, inc=1, device_id=(seq, z_up), device_id_type=MESH)

    def head_of(shape, axis):
        return lax.shift_right_logical(iota(shape, axis), HEAD.bit_length() - 1)

    lane_heads = heads.bit_length() - 1
    one = ((iota((kh, width), 0) & (heads - 1)) == head_of((kh, width), 1)).astype(BF16)
    spread[0:kh, :] = one
    spread[kh:2 * kh, :] = one
    tri = (iota((q, q), 0) >= iota((q, q), 1)).astype(BF16)
    tri3 = jnp.concatenate([tri] * 3, axis=1)
    own_row = lax.shift_right_logical(iota((nc, kh), 1), lane_heads) == iota((nc, kh), 0)
    lane_chunk = lax.shift_right_logical(iota((q, 2 * kh), 1) & (kh - 1), lane_heads)

    whole_load(2).wait()
    stacked = jnp.concatenate([ld_ref[:, c * q:(c + 1) * q] for c in range(nc)], axis=0)
    cum = nt(tri3, pieces(stacked, 3, 1))
    rho = cum[q // 2 - 1:q // 2, :]
    tot = cum[q - 1:q, :]
    shifted = cum - rho
    parts_i[...] = pieces(jnp.exp(-shifted), 2, 1)
    parts_a[...] = pieces(jnp.exp(shifted), 2, 1)

    def by_chunk(parts):
        return jnp.concatenate(
            [jnp.where(lane_chunk == c, parts[...], jnp.zeros((), BF16)) for c in range(nc)], axis=0)

    inv_exp[...] = nn(by_chunk(parts_i), spread[...])
    pair_rows = jnp.concatenate(
        [jnp.where(own_row, jnp.exp(rho), 0.0), jnp.where(own_row, jnp.exp(tot - rho), 0.0)], axis=0)
    rows[...] = nn(pieces(pair_rows, 3, 1), jnp.concatenate([one, one, one], axis=0))
    both = rows[0:nc, :] * rows[nc:2 * nc, :]
    total = both[0:1, :]
    for c in range(1, nc):
        total = total * both[c:c + 1, :]
    for h in range(2):
        for r in range(lb):
            lamh[h, r:r + 1, :] = total[:, h * half + r * LANES:h * half + (r + 1) * LANES]

    def fwd_local(c):
        if c % (nc // 4) == 0:
            loads(0, c // (nc // 4)).wait()
        rc = slice(c * q, (c + 1) * q)
        scaled = (xv[rc, :].astype(F32) * inv_exp[rc, :]).astype(BF16)
        xs[c] = scaled
        got = tn(b_ref[rc, :], scaled)
        gmat[c] = got
        f = rows[c:c + 1, :]
        g = rows[nc + c:nc + c + 1, :]
        state[...] = g * got if c == 0 else g * (f * state[...] + got)

    def bwd_local(c):
        if (c + 1) % (nc // 4) == 0:
            loads(1, c // (nc // 4)).wait()
        rc = slice(c * q, (c + 1) * q)
        scaled = (dyv[rc, :].astype(F32) * a_exp[rc, :]).astype(BF16)
        ds[c] = scaled
        got = tn(c_ref[rc, :], scaled)
        hmat[c] = got
        f = rows[c:c + 1, :]
        g = rows[nc + c:nc + c + 1, :]
        grad[...] = f * got if c == nc - 1 else f * (g * grad[...] + got)

    def to_halves(src, dst):
        for h in range(2):
            for r in range(lb):
                lo = h * half + r * LANES
                dst[h, :, r * pr:(r + 1) * pr, :] = src[:, lo:lo + LANES].reshape(chips, pr, LANES)

    first = core == 0

    def piece_of(d):
        return chip_to(d) if d < count else chip

    def pair_send(base, src, dst, which):
        out = []
        for d in range(count + 1):
            p = which(d)
            out.append(remote(src.at[p], dst.at[p], pair_s.at[base, d], pair_r.at[base, d], partner))
            out[-1].start()
        return out

    def pass_on(base, d, src, dst, p):
        span = pl.ds(0, lb * pr + (lb if base == 0 else 0))
        copy = remote(src.at[p, span], dst.at[chip, span], a2a_s.at[base, d], a2a_r.at[base, d], chip_dev(p))
        copy.start()
        return copy

    def lam_rows():
        return ([lamh[core, r:r + 1, :] for r in range(lb)], [lamp[r:r + 1, :] for r in range(lb)])

    def combine(base, came, kept, got, out, dst, forward):
        lo_, lp_ = lam_rows()
        go = []
        for d in range(count + 1):
            p = piece_of(d)
            came[d].wait_recv()
            for r in range(lb):
                lanes = slice(r * pr, (r + 1) * pr)
                mine, theirs = kept[core, p, lanes, :], got[p, lanes, :]
                if forward:
                    value = jnp.where(first, lp_[r], 1.0) * mine + jnp.where(first, 1.0, lo_[r]) * theirs
                else:
                    value = jnp.where(first, 1.0, lp_[r]) * mine + jnp.where(first, lo_[r], 1.0) * theirs
                if d < count:
                    out[p, lanes, :] = value
                else:
                    dst[chip, lanes, :] = value
            if forward:
                for r in range(lb):
                    row = slice(lb * pr + r, lb * pr + r + 1)
                    if d < count:
                        out[p, row, :] = lo_[r] * lp_[r]
                    else:
                        dst[chip, row, :] = lo_[r] * lp_[r]
            if d < count:
                go.append(pass_on(base, d, out, dst, p))
        return go

    def scan_pieces(go, base, got, out, dst, order):
        for copy in go:
            copy.wait_recv()
        run = [jnp.zeros((pr, LANES), F32) for _ in range(lb)]
        for p in order:
            for r in range(lb):
                out[p, r * pr:(r + 1) * pr, :] = run[r]
                run[r] = rf[p, lb * pr + r:lb * pr + r + 1, :] * run[r] + got[p, r * pr:(r + 1) * pr, :]
        dst[chip] = out[chip]
        return [pass_on(base, d, out, dst, chip_to(d)) for d in range(count)]

    def place(dst, p, r, lane_half, value):
        lo = pl.multiple_of(lane_half * half + r * LANES, LANES)
        dst[pl.ds(pl.multiple_of(p * pr, pr), pr), pl.ds(lo, LANES)] = value

    def hand_out(base, ret, enters, kept, got, share, shared, dst, forward):
        lo_, lp_ = lam_rows()
        out = []
        for d in [count, *range(count)]:
            p = chip_from(d) if d < count else chip
            if d < count:
                ret[d].wait_recv()
            for r in range(lb):
                lanes = slice(r * pr, (r + 1) * pr)
                enter = enters[p, lanes, :]
                if forward:
                    past = jnp.where(first, lo_[r], lp_[r]) * enter + jnp.where(
                        first, kept[core, p, lanes, :], got[p, lanes, :])
                    own, theirs = jnp.where(first, enter, past), jnp.where(first, past, enter)
                else:
                    past = jnp.where(first, lp_[r], lo_[r]) * enter + jnp.where(
                        first, got[p, lanes, :], kept[core, p, lanes, :])
                    own, theirs = jnp.where(first, past, enter), jnp.where(first, enter, past)
                share[p, lanes, :] = theirs
                place(dst, p, r, core, own)
            copy = remote(share.at[p], shared.at[p], pair_s.at[base, d], pair_r.at[base, d], partner)
            copy.start()
            out.append((p, copy))
        return out

    def take_in(pairs, shared, dst):
        for p, copy in pairs:
            copy.wait_recv()
            for r in range(lb):
                place(dst, p, r, other, shared[p, r * pr:(r + 1) * pr, :])

    lower = iota((q, q), 0) >= iota((q, q), 1)
    upper = iota((q, q), 0) <= iota((q, q), 1)

    def inner(c):
        rc = slice(c * q, (c + 1) * q)
        bb, cc = b_ref[rc, :], c_ref[rc, :]
        mm[c] = jnp.where(lower, nt(cc, bb), 0.0).astype(BF16)
        mt[c] = jnp.where(upper, nt(bb, cc), 0.0).astype(BF16)
        dm = jnp.where(lower, nt(ds[c], xs[c]), 0.0).astype(BF16)
        dcs[c] = nn(dm, bb)
        dbs[c] = tn(dm, cc)

    whole_load(0).wait()
    for c in range(nc):
        fwd_local(c)
    to_halves(state, th)
    pl.semaphore_wait(barrier, chips + 2)
    send_lam = remote(lamh.at[other], lamp, lam_s, lam_r, partner)
    send_lam.start()
    pair_f = pair_send(0, th.at[other], pf, piece_of)
    whole_load(1).wait()
    a_exp[...] = nn(by_chunk(parts_a), spread[...])
    for c in reversed(range(nc)):
        bwd_local(c)
    to_halves(grad, tb)
    pair_b = pair_send(1, tb.at[other], pb, piece_of)
    whole_load(3).wait()
    send_lam.wait_recv()
    go_f = combine(0, pair_f, th, pf, cmf, rf, True)
    go_b = combine(1, pair_b, tb, pb, cmb, rb, False)
    for c in range(nc // 2):
        inner(c)
    ret_f = scan_pieces(go_f, 2, rf, esf, ref_, range(chips))
    for c in range(nc // 2, 3 * nc // 4):
        inner(c)
    ret_b = scan_pieces(go_b, 3, rb, esb, reb, list(reversed(range(chips))))
    for c in range(3 * nc // 4, nc):
        inner(c)
    tri_s[...] = jnp.concatenate([tri] * 3, axis=0)
    head_one = (head_of((heads, width), 1) == iota((heads, width), 0)).astype(BF16)
    skipe[...] = nn(pieces(skip_ref[...], 3, 1), jnp.concatenate([head_one] * 3, axis=0))
    col = (head_of((width, heads), 0) == iota((width, heads), 1)).astype(BF16)
    heads_of[...] = jnp.concatenate([col, col], axis=0)
    send_2f = hand_out(2, ret_f, ref_, th, pf, p2f, pef, state, True)
    take_in(send_2f, pef, state)

    for c in range(nc):
        entering = rows[c:c + 1, :] * state[...]
        sp[c] = entering.astype(BF16)
        leaving = entering + gmat[c]
        gmat[c] = leaving
        state[...] = rows[nc + c:nc + c + 1, :] * leaving

    hq = q // 2
    started = {}

    def chunk_at(way, step):
        gap = far - step
        return lax.rem(z + (ring - gap if way == 0 else gap), ring)

    def rs_send(t, own, way, step, long):
        lo = (way if long else 1 - way) * hq
        first_step = 0 if long else 1
        k = chunk_at(way, step)
        if step == first_step:
            src = own.at[k, pl.ds(lo, hq)]
        else:
            started[t, way, step - 1, long].wait_recv()
            rsbuf[t, way, step - 1, lo:lo + hq, :] += own[k, lo:lo + hq, :]
            src = rsbuf.at[t, way, step - 1, pl.ds(lo, hq)]
        copy = remote(src, rsbuf.at[t, way, step, pl.ds(lo, hq)],
                      rs_s.at[t, way, step, int(long)], rs_r.at[t, way, step, int(long)],
                      (seq, z_dn if way == 0 else z_up))
        copy.start()
        started[t, way, step, long] = copy

    def rs_poll(t, own, step):
        for way in range(2):
            rs_send(t, own, way, step, True)
        if step + 1 < far:
            for way in range(2):
                rs_send(t, own, way, step + 1, False)

    def rs_end(t, own, out):
        for way in range(2):
            for long in (False, True):
                started[t, way, far - 1, long].wait_recv()
        out[...] = own[z] + rsbuf[t, 0, far - 1] + rsbuf[t, 1, far - 1]

    def near(i):
        gap = far - (i + 1) // 2
        return lax.rem(z + (gap if i % 2 == 1 else ring - gap), ring)

    def dc_chunk(i):
        c = near(i)
        dcs[c] += nt(ds[c], sp[c])

    def db_chunk(i):
        c = near(i)
        dbs[c] += nt(xs[c], tp[c])

    send_2b = hand_out(3, ret_b, reb, tb, pb, p2b, peb, grad, False)
    for i in range(3):
        dc_chunk(i)
    rs_poll(0, dcs, 0)
    for i in range(3, min(5, nc)):
        dc_chunk(i)
    take_in(send_2b, peb, grad)

    for c in reversed(range(nc)):
        later = rows[nc + c:nc + c + 1, :] * grad[...]
        low = later.astype(BF16)
        tp[c] = low
        bnd[c:c + 1, :] = jnp.sum(low.astype(F32) * gmat[c], axis=0, keepdims=True)
        if c:
            grad[...] = rows[c:c + 1, :] * (later + hmat[c])
    for i in range(3):
        db_chunk(i)
    rs_poll(1, dbs, 0)
    for i in range(5, nc):
        dc_chunk(i)
    for i in range(3, nc):
        db_chunk(i)
    rs_poll(0, dcs, 1)

    last_row = iota((q, width), 0) == q - 1

    def outputs(c):
        rc = slice(c * q, (c + 1) * q)
        x_c, d_c = xs[c], ds[c]
        acc_y = nn(jnp.concatenate([mm[c], c_ref[rc, :]], axis=1),
                   jnp.concatenate([x_c, sp[c]], axis=0))
        acc_x = nn(jnp.concatenate([mt[c], b_ref[rc, :]], axis=1),
                   jnp.concatenate([d_c, tp[c]], axis=0))
        gain = skipe[...]
        y_ref[rc, :] = (a_exp[rc, :] * acc_y + gain * xv[rc, :].astype(F32)).astype(BF16)
        dx_ref[rc, :] = (inv_exp[rc, :] * acc_x + gain * dyv[rc, :].astype(F32)).astype(BF16)
        diff = d_c.astype(F32) * acc_y - x_c.astype(F32) * acc_x
        diff = diff + jnp.where(last_row, bnd[c:c + 1, :], 0.0)
        per_head = nn(pieces(diff, 2, 1), heads_of[...])
        gld_ref[:, rc] = tn(pieces(per_head, 3, 0), tri_s[...])

    done = 0
    for step in range(1, far):
        upto = nc * step // far
        for c in range(done, upto):
            outputs(c)
        done = upto
        rs_poll(1, dbs, step)
        if step + 1 < far:
            rs_poll(0, dcs, step + 1)
    for c in range(done, nc):
        outputs(c)
    rs_end(0, dcs, gc_ref)
    rs_end(1, dbs, gb_ref)
    for copy in [send_lam, *pair_f, *pair_b, *go_f, *go_b, *ret_f, *ret_b,
                 *[c for _, c in send_2f], *[c for _, c in send_2b], *started.values()]:
        copy.wait_send()


def finish_kernel(*refs):
    count = (len(refs) - 1) // 2
    sems = refs[-1]
    copies = []
    for k in range(count):
        src, dst = refs[k], refs[count + k]
        parts = 4 if src.shape[0] >= 1024 else 1
        size = src.shape[0] // parts
        for i in range(parts):
            rows = pl.ds(i * size, size)
            copies.append(pltpu.make_async_copy(src.at[rows], dst.at[rows], sems.at[k, i]))
    for copy in copies:
        copy.start()
    for copy in copies:
        copy.wait()


def finish(arrays):
    return pl.pallas_call(
        finish_kernel,
        out_shape=tuple(jax.ShapeDtypeStruct(a.shape, a.dtype) for a in arrays),
        in_specs=[pl.BlockSpec(memory_space=pltpu.VMEM)] * len(arrays),
        out_specs=(pl.BlockSpec(memory_space=pl.ANY),) * len(arrays),
        scratch_shapes=[pltpu.SemaphoreType.DMA((len(arrays), 4))],
        compiler_params=pltpu.CompilerParams(vmem_limit_bytes=16 * 1024 * 1024),
    )(*arrays)


def body(chips, ring, mixer_input, log_decay, b_rows, c_rows, skip_gain, grad_out):
    length, width = mixer_input.shape
    heads = log_decay.shape[0]
    state_n = b_rows.shape[1]
    nc = ring
    q = length // nc
    kh = nc * heads
    pr = state_n // chips
    lb = width // 2 // LANES
    far = ring // 2
    vm = pltpu.VMEM
    msg = (chips, lb * pr, LANES)
    msg_l = (chips, lb * pr + 8, LANES)
    scratch = [
        vm((length, width), BF16), vm((length, width), BF16),
        vm((length, state_n), BF16), vm((length, state_n), BF16),
        vm((heads, length), F32), vm((1, heads), F32),
        vm((nc, q, width), BF16), vm((nc, q, width), BF16),
        vm((length, width), F32), vm((length, width), F32),
        vm((nc, state_n, width), F32), vm((nc, state_n, width), F32),
        vm((nc, state_n, width), BF16), vm((nc, state_n, width), BF16),
        vm((nc, q, q), BF16), vm((nc, q, q), BF16),
        vm((nc, q, state_n), F32), vm((nc, q, state_n), F32),
        vm((nc, width), F32),
        vm((2 * kh, width), BF16), vm((q, 2 * kh), BF16), vm((q, 2 * kh), BF16),
        vm((2 * nc, width), F32), vm((2 * width, heads), BF16), vm((3 * q, q), BF16), vm((1, width), F32),
        vm((state_n, width), F32), vm((state_n, width), F32),
        vm((2, *msg), F32), vm((2, *msg), F32), vm((2, 8, LANES), F32), vm((8, LANES), F32),
        vm(msg, F32), vm(msg, F32),
        vm(msg_l, F32), vm(msg, F32), vm(msg_l, F32), vm(msg, F32), vm(msg, F32), vm(msg, F32),
        vm(msg, F32), vm(msg, F32), vm(msg, F32), vm(msg, F32), vm(msg, F32), vm(msg, F32),
        vm((2, 2, far, q, state_n), F32),
        pltpu.SemaphoreType.DMA((2, 6)),
        pltpu.SemaphoreType.DMA, pltpu.SemaphoreType.DMA,
        pltpu.SemaphoreType.DMA((4, chips)), pltpu.SemaphoreType.DMA((4, chips)),
        pltpu.SemaphoreType.DMA((4, chips)), pltpu.SemaphoreType.DMA((4, chips)),
        pltpu.SemaphoreType.DMA((2, 2, far, 2)), pltpu.SemaphoreType.DMA((2, 2, far, 2)),
    ]
    whole = pl.BlockSpec(memory_space=pltpu.VMEM)
    outside = pl.BlockSpec(memory_space=pltpu.HBM)
    return finish(pl.pallas_call(
        functools.partial(kernel, chips, ring),
        out_shape=(
            vm((length, width), BF16),
            vm((length, width), BF16),
            vm((heads, length), F32),
            vm((q, state_n), F32),
            vm((q, state_n), F32),
        ),
        in_specs=[outside] * 6,
        out_specs=(whole,) * 5,
        scratch_shapes=scratch,
        compiler_params=pltpu.CompilerParams(
            collective_id=0, has_side_effects=True, vmem_limit_bytes=48 * 1024 * 1024),
    )(*[pltpu.with_memory_space_constraint(a, pltpu.HBM) for a in (
        mixer_input, log_decay, b_rows, c_rows, skip_gain.reshape(1, heads), grad_out)]))


def solution(mesh):
    chips = mesh.shape["seq"] // 2
    ring = mesh.shape["exp"]
    return jax.shard_map(
        functools.partial(body, chips, ring),
        mesh=mesh,
        in_specs=(
            P("seq", "exp"),
            P("exp", "seq"),
            P("seq", None),
            P("seq", None),
            P("exp"),
            P("seq", "exp"),
        ),
        out_specs=(
            P("seq", "exp"),
            P("seq", "exp"),
            P("exp", "seq"),
            P(("seq", "exp"), None),
            P(("seq", "exp"), None),
        ),
        check_vma=False,
    )
```
